512 devices in a mesh: gx: 32 (over z, y_hi, core), gy: 16 (over y_lo, x).
Axes of the slice: x: 4, y: 8 (y_hi: 2, y_lo: 4; y = y_hi * 4 + y_lo), z: 8, core: 2. Of those that a mesh axis runs over, the one named last changes fastest.
Arguments:
- points: float32 [2, 96, 48, 32], P(None, 'gx', 'gy'), may hold values from 0 to 1
- diffusion: float32 [96, 48, 32], P('gx', 'gy'), may hold values from 0.05 to 0.5
- drift: float32 [2, 96, 48, 32], P(None, 'gx', 'gy'), may hold values from -4 to 4
- ionization: float32 [96, 48, 32], P('gx', 'gy'), may hold values from 0.2 to 2
- source: float32 [96, 48, 32], P('gx', 'gy'), may hold values from -32 to 32
- in_weight: bfloat16 [32, 16, 2, 256], P('gx', 'gy'), may hold values from -4 to 4
- in_bias: bfloat16 [32, 16, 256], P('gx', 'gy'), may hold values from -3 to 3
- mid_weight: bfloat16 [32, 16, 256, 256], P('gx', 'gy'), may hold values from -0.375 to 0.375
- mid_bias: bfloat16 [32, 16, 256], P('gx', 'gy'), may hold values from -3 to 3
- out_weight: bfloat16 [32, 16, 256], P('gx', 'gy'), may hold values from -0.375 to 0.375
Outputs:
- dir_in_weight: float32 [32, 16, 2, 256], P('gx', 'gy')
- dir_in_bias: float32 [32, 16, 256], P('gx', 'gy')
- dir_mid_weight: float32 [32, 16, 256, 256], P('gx', 'gy')
- dir_mid_bias: float32 [32, 16, 256], P('gx', 'gy')
- dir_out_weight: float32 [32, 16, 256], P('gx', 'gy')
- loss: float32 [], replicated
The draws below stay inside these ranges and needn't reach their ends.
All inputs are finite; a program needn't handle non-finite values.
Results may differ from the reference program's by a relative error of at most 0.0012.
Values may be sent and summed in bfloat16 or wider, within the bound.
No kernel may reach another device: no remote copies, remote signals or barrier semaphores. Data moves between devices by JAX's collectives and lax.ppermute only.
A program may use at most 64 MiB of HBM per device.

```python
import math
import jax
import jax.numpy as jnp
from jax import lax

H = 256
PR = 32
SUBX = 32
SUBY = 16
RGX = 96
RGY = 48
NETS = 512


def draw_source(key, part):
    growth = jnp.exp(jnp.log(8.0) * jnp.arange(RGX, dtype=jnp.float32) / RGX)[:, None, None]
    rough = jax.random.truncated_normal(key, -4.0, 4.0, (RGX, RGY, PR), jnp.float32)
    return (growth * rough).astype(jnp.float32)


def block_scale(own_key, dims, split, low, high):
    def one(dim, blocks):
        heights = jax.random.uniform(jax.random.fold_in(jax.random.fold_in(own_key, 6), dim), (blocks,), jnp.float32, low / len(split), high / len(split))
        return jnp.repeat(jnp.exp(heights), dims[dim] // blocks).reshape((-1,) + (1,) * (len(dims) - dim - 1))

    factor_of = one(*split[0])
    for cut in split[1:]:
        factor_of = factor_of * one(*cut)
    return factor_of


def noise(own_key, shape, width, most, shards=(), kind=jnp.bfloat16):
    result = width * jax.random.normal(own_key, shape, jnp.float32)
    if shards:
        result = result * block_scale(own_key, shape, shards, -0.22, 0.18)
    return jnp.clip(result, -most, most).astype(kind)


def setup_inputs(seed: int = 0) -> dict:
    keys = jax.random.split(jax.random.key(seed), 11)
    return {
        "points": jnp.clip(1.0 * jax.random.uniform(keys[0], (2, RGX, RGY, PR), jnp.float32) ** block_scale(keys[0], (2, RGX, RGY, PR), ((1, 32), (2, 16)), -0.2, 0.2), 0.0, 1.0),
        "diffusion": jnp.clip(jnp.exp(math.log(0.5) - 2.3025851 * jax.random.uniform(keys[1], (RGX, RGY, PR), jnp.float32) ** block_scale(keys[1], (RGX, RGY, PR), ((0, 32), (1, 16)), -0.2, 0.2)), 0.05, 0.5),
        "drift": noise(keys[2], (2, RGX, RGY, PR), 1.0, 4.0, ((1, 32), (2, 16)), jnp.float32),
        "ionization": jnp.clip(jnp.exp(math.log(2.0) - 2.3025851 * jax.random.uniform(keys[3], (RGX, RGY, PR), jnp.float32) ** block_scale(keys[3], (RGX, RGY, PR), ((0, 32), (1, 16)), -0.2, 0.2)), 0.2, 2.0),
        "source": draw_source(jax.random.fold_in(keys[10], 71), 0),
        "in_weight": noise(keys[5], (SUBX, SUBY, 2, H), 1.0, 4.0, ((0, 32), (1, 16))),
        "in_bias": noise(keys[6], (SUBX, SUBY, H), 0.5, 3.0, ((0, 32), (1, 16))),
        "mid_weight": noise(keys[7], (SUBX, SUBY, H, H), H ** -0.5, 0.375, ((0, 32), (1, 16))),
        "mid_bias": noise(keys[8], (SUBX, SUBY, H), 0.5, 3.0, ((0, 32), (1, 16))),
        "out_weight": noise(keys[9], (SUBX, SUBY, H), H ** -0.5, 0.375, ((0, 32), (1, 16))),
    }


DELTA = 0.25
EPS = 1e-06

def region_frame(index):
    low = jnp.where(index == 0, 0.0, jnp.where(index == 1, DELTA, 1.0 - DELTA)).astype(jnp.float32)
    extent = jnp.where(index == 1, 1.0 - 2.0 * DELTA, DELTA).astype(jnp.float32)
    return (low, extent)

def smooth_rise(coord):
    ramp = jnp.clip((coord + DELTA) / (2.0 * DELTA), 0.0, 1.0)
    value = ramp * ramp * ramp * (10.0 - 15.0 * ramp + 6.0 * ramp * ramp)
    slope = 30.0 * ramp * ramp * (1.0 - ramp) * (1.0 - ramp) / (2.0 * DELTA)
    bend = 60.0 * ramp * (1.0 - ramp) * (1.0 - 2.0 * ramp) / (4.0 * DELTA * DELTA)
    return (value, slope, bend)

def bump(coord):
    rise_a = smooth_rise(coord)
    rise_b = smooth_rise(coord - 1.0)
    return (rise_a[0] - rise_b[0], rise_a[1] - rise_b[1], rise_a[2] - rise_b[2])

def coefficients(coord_x, coord_y, present, diff, vel_x, vel_y, rate):
    bump_x = bump(coord_x)
    bump_y = bump(coord_y)
    window = bump_x[0] * bump_y[0] * present
    window_x = bump_x[1] * bump_y[0] * present
    window_y = bump_x[0] * bump_y[1] * present
    window_l = (bump_x[2] * bump_y[0] + bump_x[0] * bump_y[2]) * present
    c_val = -diff * window_l + vel_x * window_x + vel_y * window_y - rate * window
    c_dx = -2.0 * diff * window_x + vel_x * window
    c_dy = -2.0 * diff * window_y + vel_y * window
    c_lap = -diff * window
    return (c_val, c_dx, c_dy, c_lap)

def net_state(params, coord_x, coord_y):
    w_in, b_in, w_mid, b_mid, w_out = params
    w_first = w_in[0].astype(jnp.float32)
    w_second = w_in[1].astype(jnp.float32)
    across = (2.0 * coord_x - 1.0)[:, None]
    along = (2.0 * coord_y - 1.0)[:, None]
    hid_one = jnp.tanh(across * w_first + along * w_second + b_in.astype(jnp.float32))
    damp_one = 1.0 - hid_one * hid_one
    power = w_first * w_first + w_second * w_second
    streams = jnp.concatenate([hid_one, 2.0 * damp_one * w_first, 2.0 * damp_one * w_second, -8.0 * hid_one * damp_one * power], axis=0).astype(jnp.bfloat16)
    mixed = jnp.dot(streams, w_mid, preferred_element_type=jnp.float32)
    count = coord_x.shape[0]
    base = mixed[:count]
    grad_x = mixed[count:2 * count]
    grad_y = mixed[2 * count:3 * count]
    curve = mixed[3 * count:]
    hid_two = jnp.tanh(base + b_mid.astype(jnp.float32))
    damp_two = 1.0 - hid_two * hid_two
    square = grad_x * grad_x + grad_y * grad_y
    outputs = (hid_two, damp_two * grad_x, damp_two * grad_y, -2.0 * hid_two * damp_two * square + damp_two * curve)
    return dict(across=across, along=along, hid_one=hid_one, damp_one=damp_one, power=power, streams=streams, grad_x=grad_x, grad_y=grad_y, curve=curve, hid_two=hid_two, damp_two=damp_two, square=square, outputs=outputs, w_first=w_first, w_second=w_second)

def net_fields(params, coord_x, coord_y):
    state = net_state(params, coord_x, coord_y)
    head = params[4].astype(jnp.float32)
    return tuple((jnp.dot(out_k, head, precision=lax.Precision.HIGHEST) for out_k in state['outputs']))

def combine(factors, fields):
    return factors[0] * fields[0] + factors[1] * fields[1] + factors[2] * fields[2] + factors[3] * fields[3]

def net_backward(params, coord_x, coord_y, cots):
    state = net_state(params, coord_x, coord_y)
    w_mid = params[2]
    head = params[4].astype(jnp.float32)
    outputs = state['outputs']
    d_out = jnp.dot(cots[0], outputs[0], precision=lax.Precision.HIGHEST)
    for index in range(1, 4):
        d_out = d_out + jnp.dot(cots[index], outputs[index], precision=lax.Precision.HIGHEST)
    d_o = [cot_k[:, None] * head for cot_k in cots]
    hid_two = state['hid_two']
    damp_two = state['damp_two']
    square = state['square']
    grad_x = state['grad_x']
    grad_y = state['grad_y']
    d_damp = d_o[1] * grad_x + d_o[2] * grad_y + (-2.0 * hid_two * square + state['curve']) * d_o[3]
    d_hid = d_o[0] - 2.0 * damp_two * square * d_o[3] - 2.0 * hid_two * d_damp
    d_base = d_hid * damp_two
    d_gx = d_o[1] * damp_two - 4.0 * hid_two * damp_two * grad_x * d_o[3]
    d_gy = d_o[2] * damp_two - 4.0 * hid_two * damp_two * grad_y * d_o[3]
    d_curve = damp_two * d_o[3]
    d_bmid = lax.optimization_barrier(jnp.sum(d_base, axis=0))
    d_mixed = jnp.concatenate([d_base, d_gx, d_gy, d_curve], axis=0).astype(jnp.bfloat16)
    d_wmid = lax.dot_general(state['streams'], d_mixed, (((0,), (0,)), ((), ())), preferred_element_type=jnp.float32)
    d_streams = lax.dot_general(d_mixed, w_mid, (((1,), (1,)), ((), ())), preferred_element_type=jnp.float32)
    count = coord_x.shape[0]
    ds_zero = d_streams[:count]
    ds_one = d_streams[count:2 * count]
    ds_two = d_streams[2 * count:3 * count]
    ds_three = d_streams[3 * count:]
    hid_one = state['hid_one']
    damp_one = state['damp_one']
    power = state['power']
    w_first = state['w_first']
    w_second = state['w_second']
    d_damp1 = 2.0 * w_first * ds_one + 2.0 * w_second * ds_two - 8.0 * hid_one * power * ds_three
    d_hid1 = ds_zero - 8.0 * damp_one * power * ds_three - 2.0 * hid_one * d_damp1
    d_pre = d_hid1 * damp_one
    d_first = lax.optimization_barrier(jnp.sum(2.0 * damp_one * ds_one - 16.0 * hid_one * damp_one * w_first * ds_three + state['across'] * d_pre, axis=0))
    d_second = lax.optimization_barrier(jnp.sum(2.0 * damp_one * ds_two - 16.0 * hid_one * damp_one * w_second * ds_three + state['along'] * d_pre, axis=0))
    d_bin = lax.optimization_barrier(jnp.sum(d_pre, axis=0))
    return (jnp.stack([d_first, d_second], axis=0), d_bin, d_wmid, d_bmid, d_out)

def pad_cells(array):
    wrapped = jnp.concatenate([array[..., -1:, :], array, array[..., :1, :]], axis=-2)
    widths = [(0, 0)] * (array.ndim - 3) + [(1, 1), (0, 0), (0, 0)]
    return jnp.pad(wrapped, widths)

def reference(points, diffusion, drift, ionization, source, in_weight, in_bias, mid_weight, mid_bias, out_weight):
    low_x, width_x = region_frame(jnp.arange(RGX, dtype=jnp.int32) % 3)
    low_y, width_y = region_frame(jnp.arange(RGY, dtype=jnp.int32) % 3)
    pos_x = low_x[:, None, None] + width_x[:, None, None] * points[0]
    pos_y = low_y[None, :, None] + width_y[None, :, None] * points[1]
    area = width_x[:, None, None] * width_y[None, :, None] / PR * jnp.ones_like(pos_x)
    stacked = jnp.stack([pos_x, pos_y, diffusion, drift[0], drift[1], ionization], axis=0)
    padded = pad_cells(stacked)
    shift_int = jnp.array([-1, 0, 0, 0, 1], dtype=jnp.int32)
    shift_float = shift_int.astype(jnp.float32)
    zero_index = jnp.zeros((), jnp.int32)

    def cycle_of(number):
        cell_x = (number // SUBY).astype(jnp.int32)
        cell_y = (number % SUBY).astype(jnp.int32)
        cycle_data = lax.dynamic_slice(padded, (zero_index, 3 * cell_x, 3 * cell_y, zero_index), (6, 5, 5, PR))
        coord_x = cycle_data[0] + shift_float[:, None, None]
        coord_y = cycle_data[1] + shift_float[None, :, None]
        owner = cell_x + shift_int
        present = ((owner >= 0) & (owner < SUBX)).astype(jnp.float32)[:, None, None] * jnp.ones_like(coord_x)
        factors = coefficients(coord_x, coord_y, present, cycle_data[2], cycle_data[3], cycle_data[4], cycle_data[5])
        params = (in_weight[cell_x, cell_y], in_bias[cell_x, cell_y], mid_weight[cell_x, cell_y], mid_bias[cell_x, cell_y], out_weight[cell_x, cell_y])
        return (cell_x, cell_y, coord_x.reshape(-1), coord_y.reshape(-1), tuple((f.reshape(-1) for f in factors)), params)

    def forward_step(totals, number):
        cell_x, cell_y, coord_x, coord_y, factors, params = cycle_of(number)
        contrib = combine(factors, net_fields(params, coord_x, coord_y)).reshape(5, 5, PR)
        corner = (3 * cell_x, 3 * cell_y, zero_index)
        current = lax.dynamic_slice(totals, corner, (5, 5, PR))
        return (lax.dynamic_update_slice(totals, current + contrib, corner), None)
    numbers = jnp.arange(NETS, dtype=jnp.int32)
    totals, _ = lax.scan(forward_step, jnp.zeros((RGX + 2, RGY + 2, PR), jnp.float32), numbers)
    inner = totals[1:-1, 1:-1]
    inner = inner.at[:, 0].add(totals[1:-1, -1]).at[:, -1].add(totals[1:-1, 0])
    residual = inner - source
    loss = jnp.sum(area * residual * residual)
    adjoint = 2.0 * area * residual
    adjoint_pad = pad_cells(adjoint)

    def grads_of(number):
        cell_x, cell_y, coord_x, coord_y, factors, params = cycle_of(number)
        weights_here = lax.dynamic_slice(adjoint_pad, (3 * cell_x, 3 * cell_y, zero_index), (5, 5, PR)).reshape(-1)
        cots = tuple((weights_here * f for f in factors))
        return net_backward(params, coord_x, coord_y, cots)
    grads = lax.map(grads_of, numbers)
    grads = tuple((g.reshape((SUBX, SUBY) + g.shape[1:]) for g in grads))
    square = jnp.sum(grads[0] * grads[0])
    for index in range(1, 5):
        square = square + jnp.sum(grads[index] * grads[index])
    rms = jnp.sqrt(square / (NETS * (H * H + 5 * H)) + EPS)
    return (grads[0] / rms, grads[1] / rms, grads[2] / rms, grads[3] / rms, grads[4] / rms, loss)
```

```python
import jax
import jax.numpy as jnp
from jax import lax
from jax.experimental import pallas as pl
from jax.experimental.pallas import tpu as pltpu
from jax.sharding import Mesh, PartitionSpec as P

DELTA = 0.25
EPS = 1e-06
H = 256
LANES = 128
SPAN = 32
ROWS = 288
F32 = jnp.float32
BF16 = jnp.bfloat16

CHUNKS = (
    ((0, 0), (0, 1), (1, 0), (1, 1)),
    ((0, 3), (0, 4), (1, 3), (1, 4)),
    ((3, 0), (3, 1), (4, 0), (4, 1)),
    ((3, 3), (3, 4), (4, 3), (4, 4)),
    ((0, 2), (1, 2), (3, 2), (4, 2)),
    ((2, 0), (2, 1), (2, 3), (2, 4)),
    ((2, 2),),
)
PLACE = {
    (0, 0): 0,
    (0, 1): 32,
    (0, 2): 64,
    (1, 0): 96,
    (2, 0): 128,
    (2, 1): 160,
    (2, 2): 192,
    (1, 2): 224,
    (1, 1): 256,
}
LOW = (0.0, DELTA, 1.0 - DELTA)
WIDTH = (DELTA, 1.0 - 2.0 * DELTA, DELTA)


def smooth_rise(coord):
    ramp = jnp.clip((coord + DELTA) / (2.0 * DELTA), 0.0, 1.0)
    value = ramp * ramp * ramp * (10.0 - 15.0 * ramp + 6.0 * ramp * ramp)
    slope = 30.0 * ramp * ramp * (1.0 - ramp) * (1.0 - ramp) / (2.0 * DELTA)
    bend = 60.0 * ramp * (1.0 - ramp) * (1.0 - 2.0 * ramp) / (4.0 * DELTA * DELTA)
    return (value, slope, bend)


def bump(coord):
    rise_a = smooth_rise(coord)
    rise_b = smooth_rise(coord - 1.0)
    return (rise_a[0] - rise_b[0], rise_a[1] - rise_b[1], rise_a[2] - rise_b[2])


def pack_kernel(
    pts, dif, dri, ion, src, w_in, b_in, w_mid, b_mid, w_out, pay_ref, tab_ref
):
    zeros = jnp.zeros((1, SPAN), F32)
    ones = jnp.ones((1, SPAN), F32)
    pieces = {}
    for a in range(3):
        for b in range(3):
            rows = [
                LOW[a] + WIDTH[a] * pts[0, a, b : b + 1, :],
                LOW[b] + WIDTH[b] * pts[1, a, b : b + 1, :],
                dif[a, b : b + 1, :],
                dri[0, a, b : b + 1, :],
                dri[1, a, b : b + 1, :],
                ion[a, b : b + 1, :],
                src[a, b : b + 1, :],
                ones,
            ]
            pieces[PLACE[a, b]] = jnp.concatenate(rows, axis=0)
    blank = jnp.concatenate([zeros] * 8, axis=0)
    order = [pieces.get(32 * k, blank) for k in range(12)]
    tabs = [jnp.concatenate(order[4 * k : 4 * k + 4], axis=1) for k in range(3)]
    for k in range(3):
        tab_ref[:, 128 * k : 128 * k + 128] = tabs[k]
    edge = jnp.concatenate(tabs[:2], axis=1)
    high = edge.astype(BF16).astype(F32)
    rest = edge - high
    mid = rest.astype(BF16).astype(F32)
    low = rest - mid
    small = jnp.concatenate(
        [
            w_in[0, 0].astype(F32),
            b_in[0].astype(F32),
            b_mid[0].astype(F32),
            w_out[0].astype(F32),
            jnp.ones((1, H), F32),
            jnp.zeros((2, H), F32),
        ],
        axis=0,
    )
    pay_ref[H:ROWS, :] = jnp.concatenate([high, mid, low, small], axis=0).astype(BF16)
    pay_ref[0:H, :] = jnp.transpose(w_mid[0, 0].astype(F32)).astype(BF16)


def small_rows(ref, index):
    return ref[index, H:ROWS, :].astype(F32)


def columns_of(small):
    w_first, w_second = small[24:25], small[25:26]
    power = w_first * w_first + w_second * w_second
    rows = jnp.concatenate(
        [
            w_first,
            w_second,
            small[26:27],
            2.0 * w_first,
            2.0 * w_second,
            -8.0 * power,
            small[27:28],
            small[28:29],
        ],
        axis=0,
    )
    return jnp.transpose(rows)


def forward(cols, weights, xi, eta):
    h1 = jnp.tanh(xi * cols[:, 0:1] + eta * cols[:, 1:2] + cols[:, 2:3])
    d1 = 1.0 - h1 * h1
    streams = jnp.concatenate(
        [
            h1.astype(BF16),
            (d1 * cols[:, 3:4]).astype(BF16),
            (d1 * cols[:, 4:5]).astype(BF16),
            (h1 * d1 * cols[:, 5:6]).astype(BF16),
        ],
        axis=1,
    )
    mixed = jnp.dot(weights, streams, preferred_element_type=F32)
    h2 = jnp.tanh(mixed[:, 0:LANES] + cols[:, 6:7])
    gx = mixed[:, LANES : 2 * LANES]
    gy = mixed[:, 2 * LANES : 3 * LANES]
    curve = mixed[:, 3 * LANES :]
    return h1, streams, h2, gx, gy, curve


def output_mix(c, h2, gx, gy, curve):
    d2 = 1.0 - h2 * h2
    square = gx * gx + gy * gy
    return c[0] * h2 + d2 * (
        c[1] * gx + c[2] * gy + c[3] * (curve - 2.0 * h2 * square)
    )


def select(step, values):
    out = jnp.int32(values[0])
    for k in range(1, len(values)):
        out = jnp.where(step == k, jnp.int32(values[k]), out)
    return out


def net_kernel(
    mid_ref,
    lo_ref,
    hi_ref,
    tab_ref,
    w_ref,
    gw_ref,
    gs_ref,
    stat_ref,
    chunk_ref,
    coef_ref,
    total_ref,
    col_ref,
    h1_ref,
    s_ref,
    h2_ref,
    gx_ref,
    gy_ref,
    cu_ref,
    d_ref,
    acc_ref,
):
    refs = (lo_ref, mid_ref, hi_ref)
    smalls = [[small_rows(refs[q], p) for p in range(3)] for q in range(3)]
    edges = [
        [(s[0:8] + s[8:16]) + s[16:24] if (p, q) != (1, 1) else None for p, s in enumerate(row)]
        for q, row in enumerate(smalls)
    ]
    edges[1][1] = tab_ref[...]
    blank = jnp.zeros((8, SPAN), F32)
    for c, regions in enumerate(CHUNKS):
        parts = []
        for big_a, big_b in regions:
            p = 0 if big_a == 0 else 2 if big_a == 4 else 1
            q = 0 if big_b == 0 else 2 if big_b == 4 else 1
            a = (2, big_a - 1, 0)[p]
            b = (2, big_b - 1, 0)[q]
            at = PLACE[a, b]
            parts.append(edges[q][p][:, at : at + SPAN])
        parts += [blank] * (4 - len(parts))
        chunk_ref[c] = jnp.concatenate(parts, axis=1)
    chunk_ref[7] = jnp.zeros((8, LANES), F32)
    rows = [chunk_ref[:, k, :] for k in range(8)]
    pos_x, pos_y, diff, vel_x, vel_y, rate, source, flag = rows
    spot = lax.broadcasted_iota(jnp.int32, (8, LANES), 0) * 4 + (
        lax.broadcasted_iota(jnp.int32, (8, LANES), 1) // SPAN
    )

    def among(test):
        hit = jnp.zeros((8, LANES), F32)
        for c, regions in enumerate(CHUNKS):
            for k, region in enumerate(regions):
                if test(region):
                    hit = jnp.where(spot == 4 * c + k, 1.0, hit)
        return hit

    off_x = among(lambda r: r[0] == 4) - among(lambda r: r[0] == 0)
    off_y = among(lambda r: r[1] == 4) - among(lambda r: r[1] == 0)
    own = (1.0 - off_x * off_x) * (1.0 - off_y * off_y) * flag
    wide_x = DELTA + (1.0 - 3.0 * DELTA) * among(lambda r: r[0] == 2)
    wide_y = DELTA + (1.0 - 3.0 * DELTA) * among(lambda r: r[1] == 2)
    area = wide_x * wide_y / SPAN * flag
    coords_x = [pos_x + (off_x - float(p)) for p in (-1, 0, 1)]
    coords_y = [pos_y + (off_y - float(q)) for q in (-1, 0, 1)]
    bumps_x = [bump(t) for t in coords_x]
    bumps_y = [bump(s) for s in coords_y]
    for q in range(3):
        for p in range(3):
            present = smalls[q][p][29:30, 0:LANES]
            b_x, b_y = bumps_x[p], bumps_y[q]
            window = b_x[0] * b_y[0] * present
            window_x = b_x[1] * b_y[0] * present
            window_y = b_x[0] * b_y[1] * present
            window_l = (b_x[2] * b_y[0] + b_x[0] * b_y[2]) * present
            n = 3 * q + p
            coef_ref[n, 0] = 2.0 * coords_x[p] - 1.0
            coef_ref[n, 1] = 2.0 * coords_y[q] - 1.0
            coef_ref[n, 2] = (
                -diff * window_l + vel_x * window_x + vel_y * window_y - rate * window
            )
            coef_ref[n, 3] = -2.0 * diff * window_x + vel_x * window
            coef_ref[n, 4] = -2.0 * diff * window_y + vel_y * window
            coef_ref[n, 5] = -diff * window
            col_ref[n] = columns_of(smalls[q][p])
    total_ref[...] = jnp.zeros((8, LANES), F32)

    def coefs(n, c):
        return [coef_ref[n, k, pl.ds(c, 1), :] for k in range(6)]

    def add_field(c, mix, cols):
        total_ref[pl.ds(c, 1), :] += jnp.sum(mix * cols[:, 7:8], axis=0, keepdims=True)

    def sweep(q, places, chunks):
        def step(i, carry):
            p = select(i, places)
            c = select(i, chunks)
            xi, eta, *cs = coefs(3 * q + p, c)
            cols = col_ref[3 * q + p]
            _, _, h2, gx, gy, curve = forward(cols, refs[q][p, 0:H, :], xi, eta)
            add_field(c, output_mix(cs, h2, gx, gy, curve), cols)
            return carry

        lax.fori_loop(0, len(places), step, 0)

    def own_step(c, carry):
        xi, eta, *cs = coefs(4, c)
        cols = col_ref[4]
        h1, streams, h2, gx, gy, curve = forward(cols, mid_ref[1, 0:H, :], xi, eta)
        h1_ref[c] = h1
        s_ref[c] = streams
        h2_ref[c] = h2
        gx_ref[c] = gx
        gy_ref[c] = gy
        cu_ref[c] = curve
        add_field(c, output_mix(cs, h2, gx, gy, curve), cols)
        return carry

    lax.fori_loop(0, 7, own_step, 0)
    sweep(1, (0, 0, 0, 2, 2, 2), (0, 1, 4, 2, 3, 4))
    sweep(0, (0, 1, 1, 1, 2), (0, 0, 2, 5, 2))
    sweep(2, (0, 1, 1, 1, 2), (1, 1, 3, 5, 3))

    residual = total_ref[...] - source
    loss = jnp.sum(own * area * residual * residual)
    total_ref[...] = 2.0 * area * residual
    acc_ref[...] = jnp.zeros(acc_ref.shape, F32)
    gw_ref[...] = jnp.zeros((H, H), F32)

    def back_step(c, carry):
        xi, eta, *cs = coefs(4, c)
        cols = col_ref[4]
        adjoint = total_ref[pl.ds(c, 1), :]
        c0, c1, c2, c3 = (adjoint * k for k in cs)
        h1, h2, gx, gy, curve = h1_ref[c], h2_ref[c], gx_ref[c], gy_ref[c], cu_ref[c]
        acc_ref[4] += output_mix((c0, c1, c2, c3), h2, gx, gy, curve)
        head = cols[:, 7:8]
        d2 = 1.0 - h2 * h2
        square = gx * gx + gy * gy
        e0, e1, e2, e3 = c0 * head, c1 * head, c2 * head, c3 * head
        d_damp = e1 * gx + e2 * gy + (curve - 2.0 * h2 * square) * e3
        d_hid = e0 - 2.0 * d2 * square * e3 - 2.0 * h2 * d_damp
        d_base = d_hid * d2
        turn = 4.0 * h2 * d2 * e3
        acc_ref[3] += d_base
        d_ref[:, 0:LANES] = d_base.astype(BF16)
        d_ref[:, LANES : 2 * LANES] = (e1 * d2 - turn * gx).astype(BF16)
        d_ref[:, 2 * LANES : 3 * LANES] = (e2 * d2 - turn * gy).astype(BF16)
        d_ref[:, 3 * LANES :] = (d2 * e3).astype(BF16)
        d_mixed = d_ref[...]
        gw_ref[...] += lax.dot_general(
            s_ref[c], d_mixed, (((1,), (1,)), ((), ())), preferred_element_type=F32
        )
        d_streams = jnp.dot(w_ref[0, 0], d_mixed, preferred_element_type=F32)
        ds0 = d_streams[:, 0:LANES]
        ds1 = d_streams[:, LANES : 2 * LANES]
        ds2 = d_streams[:, 2 * LANES : 3 * LANES]
        ds3 = d_streams[:, 3 * LANES :]
        w1, w2, w1x2, w2x2, pw = (cols[:, k : k + 1] for k in (0, 1, 3, 4, 5))
        d1 = 1.0 - h1 * h1
        d_damp1 = w1x2 * ds1 + w2x2 * ds2 + h1 * pw * ds3
        d_hid1 = ds0 + d1 * pw * ds3 - 2.0 * h1 * d_damp1
        d_pre = d_hid1 * d1
        turn1 = 8.0 * h1 * ds3
        acc_ref[0] += 2.0 * d1 * (ds1 - turn1 * w1) + xi * d_pre
        acc_ref[1] += 2.0 * d1 * (ds2 - turn1 * w2) + eta * d_pre
        acc_ref[2] += d_pre
        return carry

    lax.fori_loop(0, 7, back_step, 0)
    sums = [jnp.sum(acc_ref[k], axis=1, keepdims=True) for k in range(5)]
    grid = jnp.concatenate(sums + [jnp.zeros((H, 3), F32)], axis=1)
    gs = jnp.transpose(grid)
    gs_ref[...] = gs
    gw = gw_ref[...]
    square = jnp.sum(gw * gw) + jnp.sum(gs * gs)
    lane = lax.broadcasted_iota(jnp.int32, stat_ref.shape, 2)
    stat_ref[...] = jnp.where(lane == 0, square, jnp.where(lane == 1, loss, 0.0))


def sum_kernel(got_ref, out_ref):
    total = jnp.sum(got_ref[...], axis=0, keepdims=True)
    out_ref[...] = jnp.broadcast_to(total, out_ref.shape)


def scale_kernel(nets, got_ref, gw_ref, gs_ref, o0, o1, o2, o3, o4, loss_ref):
    total = jnp.sum(got_ref[...], axis=0)
    rms = jnp.sqrt(total[:, 0:1] / (nets * (H * H + 5 * H)) + EPS)
    gs = gs_ref[...] / rms
    o0[0, 0] = gs[0:2]
    o1[0] = gs[2:3]
    o2[0, 0] = gw_ref[...] / rms
    o3[0] = gs[3:4]
    o4[0] = gs[4:5]
    loss_ref[...] = total[:, 1:2]


def call(kernel, outs, scratch=(), limit=16 << 20):
    return pl.pallas_call(
        kernel,
        out_shape=outs,
        scratch_shapes=scratch,
        compiler_params=pltpu.CompilerParams(vmem_limit_bytes=limit),
    )


def shape(dims, kind=F32):
    return jax.ShapeDtypeStruct(dims, kind)


GX = ("z", "yh", "c")
GY = ("yl", "x")
FIRST = ("z", "c")
SECOND = ("yh", "yl", "x")


def local(
    points,
    diffusion,
    drift,
    ionization,
    source,
    in_weight,
    in_bias,
    mid_weight,
    mid_bias,
    out_weight,
):
    count_x = lax.axis_size(GX)
    count_y = lax.axis_size(GY)
    payload, table = call(pack_kernel, (shape((ROWS, H), BF16), shape((8, 384))))(
        points,
        diffusion,
        drift,
        ionization,
        source,
        in_weight,
        in_bias,
        mid_weight,
        mid_bias,
        out_weight,
    )
    forth = [(i, i + 1) for i in range(count_x - 1)]
    back = [(i + 1, i) for i in range(count_x - 1)]
    before = lax.ppermute(payload, GX, forth)
    after = lax.ppermute(payload, GX, back)
    row = jnp.stack([before, payload, after])
    ring = [(i, (i + 1) % count_y) for i in range(count_y)]
    below = lax.ppermute(row, GY, ring)
    above = lax.ppermute(row, GY, [(j, i) for i, j in ring])
    first = lax.axis_size(FIRST)
    second = lax.axis_size(SECOND)
    state = pltpu.VMEM((7, H, LANES), F32)
    grad_w, grad_s, stat = call(
        net_kernel,
        (shape((H, H)), shape((8, H)), shape((first, 1, LANES))),
        (
            pltpu.VMEM((8, 8, LANES), F32),
            pltpu.VMEM((9, 6, 8, LANES), F32),
            pltpu.VMEM((8, LANES), F32),
            pltpu.VMEM((9, H, 8), F32),
            state,
            pltpu.VMEM((7, H, 4 * LANES), BF16),
            state,
            state,
            state,
            state,
            pltpu.VMEM((H, 4 * LANES), BF16),
            pltpu.VMEM((5, H, LANES), F32),
        ),
        limit=32 << 20,
    )(row, below, above, table, mid_weight)
    got = lax.all_to_all(stat, FIRST, 0, 0, tiled=True)
    part = call(sum_kernel, shape((second, 1, LANES)))(got)
    got = lax.all_to_all(part, SECOND, 0, 0, tiled=True)
    outs = call(
        lambda *refs: scale_kernel(count_x * count_y, *refs),
        (
            shape((1, 1, 2, H)),
            shape((1, 1, H)),
            shape((1, 1, H, H)),
            shape((1, 1, H)),
            shape((1, 1, H)),
            shape((1, 1)),
        ),
    )(got, grad_w, grad_s)
    return (*outs[:5], outs[5].reshape(()))


def solution(mesh):
    fine = Mesh(
        mesh.devices.reshape(8, 2, 2, 4, 4), ("z", "yh", "c", "yl", "x")
    )
    return jax.shard_map(
        local,
        mesh=fine,
        in_specs=(
            P(None, GX, GY, None),
            P(GX, GY, None),
            P(None, GX, GY, None),
            P(GX, GY, None),
            P(GX, GY, None),
            P(GX, GY, None, None),
            P(GX, GY, None),
            P(GX, GY, None, None),
            P(GX, GY, None),
            P(GX, GY, None),
        ),
        out_specs=(
            P(GX, GY, None, None),
            P(GX, GY, None),
            P(GX, GY, None, None),
            P(GX, GY, None),
            P(GX, GY, None),
            P(),
        ),
        check_vma=False,
    )
```

```python
import jax
import jax.numpy as jnp
from jax import lax
from jax.experimental import pallas as pl
from jax.experimental.pallas import tpu as pltpu
from jax.sharding import Mesh, PartitionSpec as P

DELTA = 0.25
EPS = 1e-06
H = 256
LANES = 128
SPAN = 32
ROWS = 288
F32 = jnp.float32
BF16 = jnp.bfloat16

MIDDLE = (
    ((0, 1), (1, 1), (0, 3), (1, 3)),
    ((3, 1), (4, 1), (3, 3), (4, 3)),
    ((0, 2), (1, 2), (3, 2), (4, 2)),
    ((2, 1), (2, 2), (2, 3)),
)
HIGH = (
    ((0, 3), (0, 4), (1, 3), (1, 4)),
    ((3, 3), (3, 4), (4, 3), (4, 4)),
    ((2, 3), (2, 4)),
    ((0, 4), (1, 4), (3, 4), (4, 4)),
)
BELOW = (
    ((0, 0), (0, 1), (1, 0), (1, 1)),
    ((3, 0), (3, 1), (4, 0), (4, 1)),
    ((2, 0), (2, 1)),
    ((0, 0), (1, 0), (3, 0), (4, 0)),
    ((2, 0), (2, 4)),
)
WINDOW = MIDDLE + (HIGH[3], BELOW[3], BELOW[4])
PLACE = {
    (0, 0): 0,
    (0, 1): 32,
    (0, 2): 64,
    (1, 0): 96,
    (2, 0): 128,
    (2, 1): 160,
    (2, 2): 192,
    (1, 2): 224,
    (1, 1): 256,
}
LOW = (0.0, DELTA, 1.0 - DELTA)
WIDTH = (DELTA, 1.0 - 2.0 * DELTA, DELTA)


def smooth_rise(coord):
    ramp = jnp.clip((coord + DELTA) / (2.0 * DELTA), 0.0, 1.0)
    value = ramp * ramp * ramp * (10.0 - 15.0 * ramp + 6.0 * ramp * ramp)
    slope = 30.0 * ramp * ramp * (1.0 - ramp) * (1.0 - ramp) / (2.0 * DELTA)
    bend = 60.0 * ramp * (1.0 - ramp) * (1.0 - 2.0 * ramp) / (4.0 * DELTA * DELTA)
    return (value, slope, bend)


def bump(coord):
    rise_a = smooth_rise(coord)
    rise_b = smooth_rise(coord - 1.0)
    return (rise_a[0] - rise_b[0], rise_a[1] - rise_b[1], rise_a[2] - rise_b[2])


def pack_kernel(*refs):
    sources, (pay_ref, tab_ref), buffers, sems = (
        refs[:10],
        refs[10:12],
        refs[12:22],
        refs[22],
    )
    pts, dif, dri, ion, src, w_in, b_in, w_mid, b_mid, w_out = buffers
    strips = [pl.ds(64 * k, 64) for k in range(4)]
    pairs = [(sources[7].at[0, 0, k], w_mid.at[0, 0, k]) for k in strips]
    pairs += [(sources[k], buffers[k]) for k in range(10) if k != 7]
    copies = [
        pltpu.make_async_copy(one, two, sems.at[k]) for k, (one, two) in enumerate(pairs)
    ]
    for copy in copies:
        copy.start()
    for copy in copies[4:]:
        copy.wait()
    zeros = jnp.zeros((1, SPAN), F32)
    ones = jnp.ones((1, SPAN), F32)
    pieces = {}
    for a in range(3):
        for b in range(3):
            rows = [
                LOW[a] + WIDTH[a] * pts[a, b, 0:1, :],
                LOW[b] + WIDTH[b] * pts[a, b, 1:2, :],
                dif[a, b : b + 1, :],
                dri[a, b, 0:1, :],
                dri[a, b, 1:2, :],
                ion[a, b : b + 1, :],
                src[a, b : b + 1, :],
                ones,
            ]
            pieces[PLACE[a, b]] = jnp.concatenate(rows, axis=0)
    blank = jnp.concatenate([zeros] * 8, axis=0)
    order = [pieces.get(32 * k, blank) for k in range(12)]
    tabs = [jnp.concatenate(order[4 * k : 4 * k + 4], axis=1) for k in range(3)]
    for k in range(3):
        tab_ref[:, 128 * k : 128 * k + 128] = tabs[k]
    edge = jnp.concatenate(tabs[:2], axis=1)
    high = edge.astype(BF16).astype(F32)
    rest = edge - high
    mid = rest.astype(BF16).astype(F32)
    low = rest - mid
    small = jnp.concatenate(
        [
            w_in[0, 0].astype(F32),
            b_in[0].astype(F32),
            b_mid[0].astype(F32),
            w_out[0].astype(F32),
            jnp.ones((1, H), F32),
            jnp.zeros((2, H), F32),
        ],
        axis=0,
    )
    pay_ref[H:ROWS, :] = jnp.concatenate([high, mid, low, small], axis=0).astype(BF16)
    for copy in copies[:4]:
        copy.wait()
    pay_ref[0:H, :] = jnp.transpose(w_mid[0, 0].astype(F32)).astype(BF16)


def small_rows(ref):
    return [ref[p, H:ROWS, :].astype(F32) for p in range(3)]


def tables(smalls):
    return [(s[0:8] + s[8:16]) + s[16:24] for s in smalls]


def gather_rows(chunk_ref, layout, points):
    blank = jnp.zeros((8, SPAN), F32)
    for c, regions in enumerate(layout):
        parts = []
        for big_a, big_b in regions:
            p = 0 if big_a == 0 else 2 if big_a == 4 else 1
            q = 0 if big_b == 0 else 2 if big_b == 4 else 1
            at = PLACE[(2, big_a - 1, 0)[p], (2, big_b - 1, 0)[q]]
            parts.append(points[q][p][:, at : at + SPAN])
        parts += [blank] * (4 - len(parts))
        chunk_ref[c] = jnp.concatenate(parts, axis=1)
    for c in range(len(layout), 8):
        chunk_ref[c] = jnp.zeros((8, LANES), F32)
    return [chunk_ref[:, k, :] for k in range(8)]


def frame(layout, flag):
    spot = lax.broadcasted_iota(jnp.int32, (8, LANES), 0) * 4 + (
        lax.broadcasted_iota(jnp.int32, (8, LANES), 1) // SPAN
    )

    def among(test):
        hit = jnp.zeros((8, LANES), F32)
        for c, regions in enumerate(layout):
            for k, region in enumerate(regions):
                if test(region):
                    hit = jnp.where(spot == 4 * c + k, 1.0, hit)
        return hit

    off_x = among(lambda r: r[0] == 4) - among(lambda r: r[0] == 0)
    off_y = among(lambda r: r[1] == 4) - among(lambda r: r[1] == 0)
    own = (1.0 - off_x * off_x) * (1.0 - off_y * off_y)
    wide_x = DELTA + (1.0 - 3.0 * DELTA) * among(lambda r: r[0] == 2)
    wide_y = DELTA + (1.0 - 3.0 * DELTA) * among(lambda r: r[1] == 2)
    return off_x, off_y, wide_x * wide_y / SPAN * flag, own


def put_coefs(coef_ref, rows, off_x, off_y, nets):
    pos_x, pos_y, diff, vel_x, vel_y, rate = rows[:6]
    coords_x = {p: pos_x + (off_x - float(p)) for p, _, _ in nets}
    coords_y = {q: pos_y + (off_y - float(q)) for _, q, _ in nets}
    bumps_x = {p: bump(t) for p, t in coords_x.items()}
    bumps_y = {q: bump(s) for q, s in coords_y.items()}
    for n, (p, q, present) in enumerate(nets):
        b_x, b_y = bumps_x[p], bumps_y[q]
        window = b_x[0] * b_y[0] * present
        window_x = b_x[1] * b_y[0] * present
        window_y = b_x[0] * b_y[1] * present
        window_l = (b_x[2] * b_y[0] + b_x[0] * b_y[2]) * present
        coef_ref[n, 0] = 2.0 * coords_x[p] - 1.0
        coef_ref[n, 1] = 2.0 * coords_y[q] - 1.0
        coef_ref[n, 2] = (
            -diff * window_l + vel_x * window_x + vel_y * window_y - rate * window
        )
        coef_ref[n, 3] = -2.0 * diff * window_x + vel_x * window
        coef_ref[n, 4] = -2.0 * diff * window_y + vel_y * window
        coef_ref[n, 5] = -diff * window


def spread(smalls, par_ref):
    lane = lax.broadcasted_iota(jnp.int32, (8, 5 * LANES), 1) // LANES
    line = lax.broadcasted_iota(jnp.int32, (8, 5 * LANES), 0)
    pick = jnp.where(lane == line, 1.0, 0.0).astype(BF16)
    for n, small in enumerate(smalls):
        wide = lax.dot_general(
            small[24:32].astype(BF16),
            pick,
            (((0,), (0,)), ((), ())),
            preferred_element_type=F32,
        )
        for k in range(5):
            par_ref[n, k] = wide[:, LANES * k : LANES * k + LANES]
        w_first, w_second = wide[:, 0:LANES], wide[:, LANES : 2 * LANES]
        par_ref[n, 5] = -8.0 * (w_first * w_first + w_second * w_second)


def forward(par_ref, n, weights, xi, eta):
    w_first, w_second = par_ref[n, 0], par_ref[n, 1]
    h1 = jnp.tanh(xi * w_first + eta * w_second + par_ref[n, 2])
    d1 = 1.0 - h1 * h1
    d1x2 = 2.0 * d1
    streams = jnp.concatenate(
        [
            h1.astype(BF16),
            (d1x2 * w_first).astype(BF16),
            (d1x2 * w_second).astype(BF16),
            (h1 * d1 * par_ref[n, 5]).astype(BF16),
        ],
        axis=1,
    )
    mixed = jnp.dot(weights, streams, preferred_element_type=F32)
    h2 = jnp.tanh(mixed[:, 0:LANES] + par_ref[n, 3])
    gx = mixed[:, LANES : 2 * LANES]
    gy = mixed[:, 2 * LANES : 3 * LANES]
    curve = mixed[:, 3 * LANES :]
    return h1, streams, h2, gx, gy, curve


def coefs(coef_ref, n, c):
    return [coef_ref[n, k, c : c + 1, :] for k in range(6)]


def add_field(total_ref, c, mix, head):
    total_ref[c : c + 1, :] += jnp.sum(mix * head, axis=0, keepdims=True)


def near_step(total_ref, coef_ref, n, c, par_ref, m, weights):
    xi, eta, c0, c1, c2, c3 = coefs(coef_ref, n, c)
    _, _, h2, gx, gy, curve = forward(par_ref, m, weights, xi, eta)
    d2 = 1.0 - h2 * h2
    square = gx * gx + gy * gy
    inner = c1 * gx + c2 * gy + c3 * (curve - 2.0 * h2 * square)
    add_field(total_ref, c, c0 * h2 + d2 * inner, par_ref[m, 4])


def own_step(total_ref, coef_ref, n, c, par_ref, weights, k, s_ref, state_ref):
    xi, eta, c0, c1, c2, c3 = coefs(coef_ref, n, c)
    h1, streams, h2, gx, gy, curve = forward(par_ref, 1, weights, xi, eta)
    d2 = 1.0 - h2 * h2
    square = gx * gx + gy * gy
    inner = c1 * gx + c2 * gy + c3 * (curve - 2.0 * h2 * square)
    mix = c0 * h2 + d2 * inner
    head = par_ref[1, 4]
    add_field(total_ref, c, mix, head)
    turn = (4.0 * c3) * h2
    s_ref[k] = streams
    state_ref[k, 0] = h1
    state_ref[k, 1] = mix
    state_ref[k, 2] = head * d2
    state_ref[k, 3] = c0 - 2.0 * (d2 * square * c3 + h2 * inner)
    state_ref[k, 4] = c1 - turn * gx
    state_ref[k, 5] = c2 - turn * gy


def middle_kernel(
    mid_ref, tab_ref, par_ref, coef_ref, info_ref, s_ref, state_ref, chunk_ref, total_ref
):
    smalls = small_rows(mid_ref)
    points = tables(smalls)
    points[1] = tab_ref[...]
    rows = gather_rows(chunk_ref, MIDDLE, [None, points, None])
    off_x, off_y, area, own = frame(MIDDLE, rows[7])
    nets = [(p - 1, 0, smalls[p][29:30, 0:LANES]) for p in range(3)]
    put_coefs(coef_ref, rows, off_x, off_y, nets)
    spread(smalls, par_ref)
    total_ref[...] = jnp.zeros((8, LANES), F32)
    for c in range(4):
        own_step(
            total_ref, coef_ref, 1, c, par_ref, mid_ref[1, 0:H, :], c, s_ref, state_ref
        )
    for p, c in ((0, 0), (2, 1), (0, 2), (2, 2)):
        near_step(total_ref, coef_ref, p, c, par_ref, p, mid_ref[p, 0:H, :])
    info_ref[0] = total_ref[...]
    info_ref[1] = area
    info_ref[2] = rows[6]
    info_ref[3] = own


def side(layout, q, mid_ref, side_ref, other, par_ref, work):
    coef_ref, total_ref, side_par, chunk_ref, s_ref, state_ref = work
    smalls = small_rows(mid_ref)
    far = small_rows(side_ref)
    points = [None, tables(smalls), None]
    points[1 + q] = tables(far)
    if other is not None:
        points[1 - q] = tables(small_rows(other))
    rows = gather_rows(chunk_ref, layout, points)
    off_x, off_y, area, _ = frame(layout, rows[7])
    nets = [(p - 1, 0, smalls[p][29:30, 0:LANES]) for p in range(3)]
    nets += [(p - 1, q, far[p][29:30, 0:LANES]) for p in range(3)]
    put_coefs(coef_ref, rows, off_x, off_y, nets)
    spread(far, side_par)
    total_ref[...] = jnp.zeros((8, LANES), F32)
    for k, c in enumerate(range(3, len(layout))):
        own_step(
            total_ref, coef_ref, 1, c, par_ref, mid_ref[1, 0:H, :], k, s_ref, state_ref
        )
    for p in (0, 2):
        near_step(total_ref, coef_ref, p, 3, par_ref, p, mid_ref[p, 0:H, :])
    for p, c in ((0, 0), (1, 0), (1, 1), (2, 1), (1, 2)):
        near_step(total_ref, coef_ref, 3 + p, c, side_par, p, side_ref[p, 0:H, :])
    return area, rows[6]


def high_kernel(
    mid_ref, hi_ref, par_ref, coef_ref, info_ref, s_ref, state_ref, side_par, chunk_ref, total_ref
):
    work = (coef_ref, total_ref, side_par, chunk_ref, s_ref, state_ref)
    area, source = side(HIGH, 1, mid_ref, hi_ref, None, par_ref, work)
    info_ref[0] = total_ref[...]
    info_ref[1] = area
    info_ref[2] = source


def moved(total, layout):
    places = {}
    for c, regions in enumerate(layout[:3]):
        for k, region in enumerate(regions):
            places[region] = (c, SPAN * k)
    rows = []
    for regions in WINDOW:
        parts = []
        for region in regions:
            if region in places:
                c, at = places[region]
                parts.append(total[c : c + 1, at : at + SPAN])
            else:
                parts.append(jnp.zeros((1, SPAN), F32))
        parts += [jnp.zeros((1, SPAN), F32)] * (4 - len(parts))
        rows.append(jnp.concatenate(parts, axis=1))
    return jnp.concatenate(rows + [jnp.zeros((1, LANES), F32)], axis=0)


def last_kernel(
    mid_ref,
    lo_ref,
    hi_ref,
    w_ref,
    par_ref,
    coef_m,
    info_m,
    s_m,
    state_m,
    coef_h,
    info_h,
    s_h,
    state_h,
    gw_ref,
    gs_ref,
    stat_ref,
    coef_l,
    s_l,
    state_l,
    side_par,
    chunk_ref,
    total_ref,
    d_ref,
    acc_ref,
):
    work = (coef_l, total_ref, side_par, chunk_ref, s_l, state_l)
    area_l, source_l = side(BELOW, -1, mid_ref, lo_ref, hi_ref, par_ref, work)
    below = total_ref[...]
    high = info_h[0]

    def joined(m, h, l):
        return jnp.concatenate(
            [m[0:4], h[3:4], l[3:5], jnp.zeros((1, LANES), F32)], axis=0
        )

    area = joined(info_m[1], info_h[1], area_l)
    source = joined(info_m[2], info_h[2], source_l)
    total = joined(info_m[0], high, below) + moved(high, HIGH) + moved(below, BELOW)
    residual = total - source
    line = lax.broadcasted_iota(jnp.int32, (8, LANES), 0)
    own = jnp.where(line < 4, info_m[3], 0.0)
    loss = jnp.sum(own * area * residual * residual)
    total_ref[...] = 2.0 * area * residual
    acc_ref[...] = jnp.zeros(acc_ref.shape, F32)
    gw_ref[...] = jnp.zeros((H, H), F32)
    w1, w2, pw = par_ref.at[1, 0], par_ref.at[1, 1], par_ref.at[1, 5]
    places = [(coef_m, c, s_m, state_m, c) for c in range(4)]
    places += [(coef_h, 3, s_h, state_h, 0), (coef_l, 3, s_l, state_l, 0)]
    places += [(coef_l, 4, s_l, state_l, 1)]
    for row, (coef_ref, c, s_ref, state_ref, k) in enumerate(places):
        xi, eta, _, _, _, c3 = coefs(coef_ref, 1, c)
        adjoint = total_ref[row : row + 1, :]
        h1 = state_ref[k, 0]
        scale = state_ref[k, 2] * adjoint
        d_base = scale * state_ref[k, 3]
        acc_ref[5] += state_ref[k, 1] * adjoint
        acc_ref[4] += d_base
        d_ref[row % 2, :, 0:LANES] = d_base.astype(BF16)
        d_ref[row % 2, :, LANES : 2 * LANES] = (scale * state_ref[k, 4]).astype(BF16)
        d_ref[row % 2, :, 2 * LANES : 3 * LANES] = (scale * state_ref[k, 5]).astype(BF16)
        d_ref[row % 2, :, 3 * LANES :] = (scale * c3).astype(BF16)
        d_mixed = d_ref[row % 2]
        d_streams = jnp.dot(w_ref[0, 0], d_mixed, preferred_element_type=F32)
        gw_ref[...] += lax.dot_general(
            s_ref[k], d_mixed, (((1,), (1,)), ((), ())), preferred_element_type=F32
        )
        ds0 = d_streams[:, 0:LANES]
        ds1 = d_streams[:, LANES : 2 * LANES]
        ds2 = d_streams[:, 2 * LANES : 3 * LANES]
        ds3 = d_streams[:, 3 * LANES :]
        d1 = 1.0 - h1 * h1
        cross = w1[...] * ds1 + w2[...] * ds2
        d_pre = d1 * (ds0 + pw[...] * ds3 * (3.0 * d1 - 2.0) - (4.0 * h1) * cross)
        d1x2 = 2.0 * d1
        acc_ref[0] += d1x2 * ds1 + xi * d_pre
        acc_ref[1] += d1x2 * ds2 + eta * d_pre
        acc_ref[2] += d_pre
        acc_ref[3] += h1 * d1 * ds3
    sums = [jnp.sum(acc_ref[k], axis=1, keepdims=True) for k in range(6)]
    turn = -16.0 * sums[3]
    grid = jnp.concatenate(
        [
            sums[0] + turn * w1[:, 0:1],
            sums[1] + turn * w2[:, 0:1],
            sums[2],
            sums[4],
            sums[5],
            jnp.zeros((H, 3), F32),
        ],
        axis=1,
    )
    gs = jnp.transpose(grid)
    gs_ref[...] = gs
    gw = gw_ref[...]
    square = jnp.sum(gw * gw) + jnp.sum(gs * gs)
    lane = lax.broadcasted_iota(jnp.int32, stat_ref.shape, 2)
    stat_ref[...] = jnp.where(lane == 0, square, jnp.where(lane == 1, loss, 0.0))


def sum_kernel(got_ref, out_ref):
    total = jnp.sum(got_ref[...], axis=0, keepdims=True)
    out_ref[...] = jnp.broadcast_to(total, out_ref.shape)


def scale_kernel(nets, got_ref, gw_ref, gs_ref, o0, o1, o2, o3, o4, loss_ref):
    total = jnp.sum(got_ref[...], axis=0)
    rms = jnp.sqrt(total[:, 0:1] / (nets * (H * H + 5 * H)) + EPS)
    gs = gs_ref[...] / rms
    o0[0, 0] = gs[0:2]
    o1[0] = gs[2:3]
    o2[0, 0] = gw_ref[...] / rms
    o3[0] = gs[3:4]
    o4[0] = gs[4:5]
    loss_ref[...] = total[:, 1:2]


def call(kernel, outs, scratch=(), limit=16 << 20, flops=0, place=pltpu.VMEM):
    extra = {}
    if place != pltpu.VMEM:
        extra["in_specs"] = [pl.BlockSpec(memory_space=place)] * 10
    return pl.pallas_call(
        kernel,
        out_shape=outs,
        scratch_shapes=scratch,
        compiler_params=pltpu.CompilerParams(vmem_limit_bytes=limit),
        cost_estimate=pl.CostEstimate(
            flops=flops, bytes_accessed=1 << 18, transcendentals=0
        ),
        **extra,
    )


def shape(dims, kind=F32):
    return jax.ShapeDtypeStruct(dims, kind)


GX = ("z", "yh", "c")
GY = ("yl", "x")
FIRST = ("z", "c")
SECOND = ("yh", "yl", "x")


def local(
    points,
    diffusion,
    drift,
    ionization,
    source,
    in_weight,
    in_bias,
    mid_weight,
    mid_bias,
    out_weight,
):
    count_x = lax.axis_size(GX)
    count_y = lax.axis_size(GY)
    inputs = (
        points.transpose(1, 2, 0, 3),
        diffusion,
        drift.transpose(1, 2, 0, 3),
        ionization,
        source,
        in_weight,
        in_bias,
        mid_weight,
        mid_bias,
        out_weight,
    )
    payload, table = call(
        pack_kernel,
        (shape((ROWS, H), BF16), shape((8, 384))),
        tuple(pltpu.VMEM(x.shape, x.dtype) for x in inputs)
        + (pltpu.SemaphoreType.DMA((13,)),),
        place=pl.ANY,
        limit=16 << 20,
    )(*(pltpu.with_memory_space_constraint(x, pltpu.HBM) for x in inputs))
    forth = [(i, i + 1) for i in range(count_x - 1)]
    back = [(i + 1, i) for i in range(count_x - 1)]
    before = lax.ppermute(payload, GX, forth)
    after = lax.ppermute(payload, GX, back)
    row = jnp.stack([before, payload, after])
    ring = [(i, (i + 1) % count_y) for i in range(count_y)]
    above = lax.ppermute(row, GY, [(j, i) for i, j in ring])
    below = lax.ppermute(row, GY, ring)
    first = lax.axis_size(FIRST)
    second = lax.axis_size(SECOND)

    def kept(chunks):
        return ((chunks, H, 4 * LANES), BF16), ((chunks, 6, H, LANES), F32)

    def outs(nets, infos, chunks):
        return (shape((nets, 6, 8, LANES)), shape((infos, 8, LANES))) + tuple(
            shape(*k) for k in kept(chunks)
        )

    chunk = pltpu.VMEM((8, 8, LANES), F32)
    total = pltpu.VMEM((8, LANES), F32)
    spreads = (3, 6, H, LANES)
    params, *middle = call(
        middle_kernel, (shape(spreads),) + outs(3, 4, 4), (chunk, total), flops=10**9
    )(row, table)
    high = call(
        high_kernel,
        outs(6, 3, 1),
        (pltpu.VMEM(spreads, F32), chunk, total),
        flops=10**9,
    )(row, above, params)
    grad_w, grad_s, stat = call(
        last_kernel,
        (shape((H, H)), shape((8, H)), shape((first, 1, LANES))),
        (
            pltpu.VMEM((6, 6, 8, LANES), F32),
            *(pltpu.VMEM(*k) for k in kept(2)),
            pltpu.VMEM(spreads, F32),
            chunk,
            total,
            pltpu.VMEM((2, H, 4 * LANES), BF16),
            pltpu.VMEM((6, H, LANES), F32),
        ),
        limit=24 << 20,
        flops=10**9,
    )(row, below, above, mid_weight, params, *middle, *high)
    got = lax.all_to_all(stat, FIRST, 0, 0, tiled=True)
    part = call(sum_kernel, shape((second, 1, LANES)))(got)
    got = lax.all_to_all(part, SECOND, 0, 0, tiled=True)
    outs = call(
        lambda *refs: scale_kernel(count_x * count_y, *refs),
        (
            shape((1, 1, 2, H)),
            shape((1, 1, H)),
            shape((1, 1, H, H)),
            shape((1, 1, H)),
            shape((1, 1, H)),
            shape((1, 1)),
        ),
    )(got, grad_w, grad_s)
    return (*outs[:5], outs[5].reshape(()))


def solution(mesh):
    fine = Mesh(
        mesh.devices.reshape(8, 2, 2, 4, 4), ("z", "yh", "c", "yl", "x")
    )
    return jax.shard_map(
        local,
        mesh=fine,
        in_specs=(
            P(None, GX, GY, None),
            P(GX, GY, None),
            P(None, GX, GY, None),
            P(GX, GY, None),
            P(GX, GY, None),
            P(GX, GY, None, None),
            P(GX, GY, None),
            P(GX, GY, None, None),
            P(GX, GY, None),
            P(GX, GY, None),
        ),
        out_specs=(
            P(GX, GY, None, None),
            P(GX, GY, None),
            P(GX, GY, None, None),
            P(GX, GY, None),
            P(GX, GY, None),
            P(),
        ),
        check_vma=False,
    )
```

```python
import functools

import jax
import jax.numpy as jnp
from jax import lax
from jax.experimental import pallas as pl
from jax.experimental.pallas import tpu as pltpu
from jax.sharding import Mesh, PartitionSpec as P

DELTA = 0.25
EPS = 1e-06
H = 256
LANES = 128
SPAN = 32
ROWS = 288
F32 = jnp.float32
BF16 = jnp.bfloat16

MIDDLE = (
    ((0, 1), (1, 1), (0, 3), (1, 3)),
    ((3, 1), (4, 1), (3, 3), (4, 3)),
    ((0, 2), (1, 2), (3, 2), (4, 2)),
    ((2, 1), (2, 2), (2, 3)),
)
HIGH = (
    ((0, 3), (0, 4), (1, 3), (1, 4)),
    ((3, 3), (3, 4), (4, 3), (4, 4)),
    ((2, 3), (2, 4)),
    ((0, 4), (1, 4), (3, 4), (4, 4)),
)
BELOW = (
    ((0, 0), (0, 1), (1, 0), (1, 1)),
    ((3, 0), (3, 1), (4, 0), (4, 1)),
    ((2, 0), (2, 1)),
    ((0, 0), (1, 0), (3, 0), (4, 0)),
    ((2, 0), (2, 4)),
)
WINDOW = MIDDLE + (HIGH[3], BELOW[3], BELOW[4])
PLACE = {
    (0, 0): 0,
    (0, 1): 32,
    (0, 2): 64,
    (1, 0): 96,
    (2, 0): 128,
    (2, 1): 160,
    (2, 2): 192,
    (1, 2): 224,
    (1, 1): 256,
}
LOW = (0.0, DELTA, 1.0 - DELTA)
WIDTH = (DELTA, 1.0 - 2.0 * DELTA, DELTA)


def smooth_rise(coord):
    ramp = jnp.clip((coord + DELTA) / (2.0 * DELTA), 0.0, 1.0)
    value = ramp * ramp * ramp * (10.0 - 15.0 * ramp + 6.0 * ramp * ramp)
    slope = 30.0 * ramp * ramp * (1.0 - ramp) * (1.0 - ramp) / (2.0 * DELTA)
    bend = 60.0 * ramp * (1.0 - ramp) * (1.0 - 2.0 * ramp) / (4.0 * DELTA * DELTA)
    return (value, slope, bend)


def bump(coord):
    rise_a = smooth_rise(coord)
    rise_b = smooth_rise(coord - 1.0)
    return (rise_a[0] - rise_b[0], rise_a[1] - rise_b[1], rise_a[2] - rise_b[2])


def pack_kernel(*refs):
    sources, (pay_ref, tab_ref), buffers, sems = (
        refs[:10],
        refs[10:12],
        refs[12:22],
        refs[22],
    )
    pts, dif, dri, ion, src, w_in, b_in, w_mid, b_mid, w_out = buffers
    strips = [pl.ds(64 * k, 64) for k in range(4)]
    pairs = [(sources[7].at[0, 0, k], w_mid.at[0, 0, k]) for k in strips]
    pairs += [(sources[k], buffers[k]) for k in range(10) if k != 7]
    copies = [
        pltpu.make_async_copy(one, two, sems.at[k]) for k, (one, two) in enumerate(pairs)
    ]
    for copy in copies:
        copy.start()
    for copy in copies[4:]:
        copy.wait()
    zeros = jnp.zeros((1, SPAN), F32)
    ones = jnp.ones((1, SPAN), F32)
    pieces = {}
    for a in range(3):
        for b in range(3):
            rows = [
                LOW[a] + WIDTH[a] * pts[a, b, 0:1, :],
                LOW[b] + WIDTH[b] * pts[a, b, 1:2, :],
                dif[a, b : b + 1, :],
                dri[a, b, 0:1, :],
                dri[a, b, 1:2, :],
                ion[a, b : b + 1, :],
                src[a, b : b + 1, :],
                ones,
            ]
            pieces[a, b] = jnp.concatenate(rows, axis=0)
    blank = jnp.concatenate([zeros] * 8, axis=0)
    turn = lax.rem(lax.axis_index("x"), 2) == 1
    placed = {
        at: jnp.where(turn, pieces[a, 2 - b], pieces[a, b]) for (a, b), at in PLACE.items()
    }
    order = [placed.get(32 * k, blank) for k in range(12)]
    tabs = [jnp.concatenate(order[4 * k : 4 * k + 4], axis=1) for k in range(3)]
    for k in range(3):
        tab_ref[:, 128 * k : 128 * k + 128] = tabs[k]
    edge = jnp.concatenate(tabs[:2], axis=1)
    high = edge.astype(BF16).astype(F32)
    rest = edge - high
    mid = rest.astype(BF16).astype(F32)
    low = rest - mid
    small = jnp.concatenate(
        [
            w_in[0, 0].astype(F32),
            b_in[0].astype(F32),
            b_mid[0].astype(F32),
            w_out[0].astype(F32),
            jnp.ones((1, H), F32),
            jnp.where(turn, -1.0, 1.0) * jnp.ones((1, H), F32),
            jnp.zeros((1, H), F32),
        ],
        axis=0,
    )
    pay_ref[H:ROWS, :] = jnp.concatenate([high, mid, low, small], axis=0).astype(BF16)
    for copy in copies[:4]:
        copy.wait()
    pay_ref[0:H, :] = jnp.transpose(w_mid[0, 0].astype(F32)).astype(BF16)


def small_rows(ref):
    return [ref[p, H:ROWS, :].astype(F32) for p in range(3)]


def tables(smalls):
    return [(s[0:8] + s[8:16]) + s[16:24] for s in smalls]


def gather_rows(chunk_ref, layout, points):
    blank = jnp.zeros((8, SPAN), F32)
    for c, regions in enumerate(layout):
        parts = []
        for big_a, big_b in regions:
            p = 0 if big_a == 0 else 2 if big_a == 4 else 1
            q = 0 if big_b == 0 else 2 if big_b == 4 else 1
            at = PLACE[(2, big_a - 1, 0)[p], (0, big_b - 1, 2)[q]]
            parts.append(points[q][p][:, at : at + SPAN])
        parts += [blank] * (4 - len(parts))
        chunk_ref[c] = jnp.concatenate(parts, axis=1)
    for c in range(len(layout), 8):
        chunk_ref[c] = jnp.zeros((8, LANES), F32)
    return [chunk_ref[:, k, :] for k in range(8)]


def frame(layout, flag):
    spot = lax.broadcasted_iota(jnp.int32, (8, LANES), 0) * 4 + (
        lax.broadcasted_iota(jnp.int32, (8, LANES), 1) // SPAN
    )

    def among(test):
        hit = jnp.zeros((8, LANES), F32)
        for c, regions in enumerate(layout):
            for k, region in enumerate(regions):
                if test(region):
                    hit = jnp.where(spot == 4 * c + k, 1.0, hit)
        return hit

    off_x = among(lambda r: r[0] == 4) - among(lambda r: r[0] == 0)
    off_y = among(lambda r: r[1] == 4) - among(lambda r: r[1] == 0)
    own = (1.0 - off_x * off_x) * (1.0 - off_y * off_y)
    wide_x = DELTA + (1.0 - 3.0 * DELTA) * among(lambda r: r[0] == 2)
    wide_y = DELTA + (1.0 - 3.0 * DELTA) * among(lambda r: r[1] == 2)
    return off_x, off_y, wide_x * wide_y / SPAN * flag, own


def put_coefs(coef_ref, rows, off_x, off_y, nets, small):
    pos_x, pos_y, diff, vel_x, vel_y, rate = rows[:6]
    way = small[30:31, 0:LANES]
    coords_x = {p: pos_x + (off_x - float(p)) for p, _, _ in nets}
    coords_y = {q: pos_y + way * (off_y - float(q)) for _, q, _ in nets}
    bumps_x = {p: bump(t) for p, t in coords_x.items()}
    bumps_y = {q: bump(s) for q, s in coords_y.items()}
    for n, (p, q, present) in enumerate(nets):
        b_x, b_y = bumps_x[p], bumps_y[q]
        window = b_x[0] * b_y[0] * present
        window_x = b_x[1] * b_y[0] * present
        window_y = b_x[0] * b_y[1] * present
        window_l = (b_x[2] * b_y[0] + b_x[0] * b_y[2]) * present
        coef_ref[n, 0] = 2.0 * coords_x[p] - 1.0
        coef_ref[n, 1] = 2.0 * coords_y[q] - 1.0
        coef_ref[n, 2] = (
            -diff * window_l + vel_x * window_x + vel_y * window_y - rate * window
        )
        coef_ref[n, 3] = -2.0 * diff * window_x + vel_x * window
        coef_ref[n, 4] = -2.0 * diff * window_y + vel_y * window
        coef_ref[n, 5] = -diff * window


def spread(smalls, par_ref):
    lane = lax.broadcasted_iota(jnp.int32, (8, 5 * LANES), 1) // LANES
    line = lax.broadcasted_iota(jnp.int32, (8, 5 * LANES), 0)
    pick = jnp.where(lane == line, 1.0, 0.0).astype(BF16)
    for n, small in enumerate(smalls):
        wide = lax.dot_general(
            small[24:32].astype(BF16),
            pick,
            (((0,), (0,)), ((), ())),
            preferred_element_type=F32,
        )
        for k in range(5):
            par_ref[n, k] = wide[:, LANES * k : LANES * k + LANES]
        w_first, w_second = wide[:, 0:LANES], wide[:, LANES : 2 * LANES]
        par_ref[n, 5] = -8.0 * (w_first * w_first + w_second * w_second)


def forward(par_ref, n, weights, xi, eta):
    w_first, w_second = par_ref[n, 0], par_ref[n, 1]
    h1 = jnp.tanh(xi * w_first + eta * w_second + par_ref[n, 2])
    d1 = 1.0 - h1 * h1
    d1x2 = 2.0 * d1
    streams = jnp.concatenate(
        [
            h1.astype(BF16),
            (d1x2 * w_first).astype(BF16),
            (d1x2 * w_second).astype(BF16),
            (h1 * d1 * par_ref[n, 5]).astype(BF16),
        ],
        axis=1,
    )
    mixed = jnp.dot(weights, streams, preferred_element_type=F32)
    h2 = jnp.tanh(mixed[:, 0:LANES] + par_ref[n, 3])
    gx = mixed[:, LANES : 2 * LANES]
    gy = mixed[:, 2 * LANES : 3 * LANES]
    curve = mixed[:, 3 * LANES :]
    return h1, streams, h2, gx, gy, curve


def coefs(coef_ref, n, c):
    return [coef_ref[n, k, c : c + 1, :] for k in range(6)]


def add_field(total_ref, c, mix, head):
    total_ref[c : c + 1, :] += jnp.sum(mix * head, axis=0, keepdims=True)


def near_step(total_ref, coef_ref, n, c, par_ref, m, weights):
    xi, eta, c0, c1, c2, c3 = coefs(coef_ref, n, c)
    _, _, h2, gx, gy, curve = forward(par_ref, m, weights, xi, eta)
    d2 = 1.0 - h2 * h2
    square = gx * gx + gy * gy
    inner = c1 * gx + c2 * gy + c3 * (curve - 2.0 * h2 * square)
    add_field(total_ref, c, c0 * h2 + d2 * inner, par_ref[m, 4])


def own_step(total_ref, coef_ref, n, c, par_ref, weights, k, s_ref, state_ref):
    xi, eta, c0, c1, c2, c3 = coefs(coef_ref, n, c)
    h1, streams, h2, gx, gy, curve = forward(par_ref, 1, weights, xi, eta)
    d2 = 1.0 - h2 * h2
    square = gx * gx + gy * gy
    inner = c1 * gx + c2 * gy + c3 * (curve - 2.0 * h2 * square)
    mix = c0 * h2 + d2 * inner
    head = par_ref[1, 4]
    add_field(total_ref, c, mix, head)
    turn = (4.0 * c3) * h2
    s_ref[k] = streams
    state_ref[k, 0] = h1
    state_ref[k, 1] = mix
    state_ref[k, 2] = head * d2
    state_ref[k, 3] = c0 - 2.0 * (d2 * square * c3 + h2 * inner)
    state_ref[k, 4] = c1 - turn * gx
    state_ref[k, 5] = c2 - turn * gy


def middle_kernel(
    mid_ref, tab_ref, par_ref, coef_ref, info_ref, s_ref, state_ref, chunk_ref, total_ref
):
    smalls = small_rows(mid_ref)
    points = tables(smalls)
    points[1] = tab_ref[...]
    rows = gather_rows(chunk_ref, MIDDLE, [None, points, None])
    off_x, off_y, area, own = frame(MIDDLE, rows[7])
    nets = [(p - 1, 0, smalls[p][29:30, 0:LANES]) for p in range(3)]
    put_coefs(coef_ref, rows, off_x, off_y, nets, smalls[1])
    spread(smalls, par_ref)
    total_ref[...] = jnp.zeros((8, LANES), F32)
    for c in range(4):
        own_step(
            total_ref, coef_ref, 1, c, par_ref, mid_ref[1, 0:H, :], c, s_ref, state_ref
        )
    for p, c in ((0, 0), (2, 1), (0, 2), (2, 2)):
        near_step(total_ref, coef_ref, p, c, par_ref, p, mid_ref[p, 0:H, :])
    info_ref[0] = total_ref[...]
    info_ref[1] = area
    info_ref[2] = rows[6]
    info_ref[3] = own


def side(layout, q, mid_ref, side_ref, other, par_ref, work):
    coef_ref, total_ref, side_par, chunk_ref, s_ref, state_ref = work
    smalls = small_rows(mid_ref)
    far = small_rows(side_ref)
    points = [None, tables(smalls), None]
    points[1 + q] = tables(far)
    if other is not None:
        points[1 - q] = tables(small_rows(other))
    rows = gather_rows(chunk_ref, layout, points)
    off_x, off_y, area, _ = frame(layout, rows[7])
    nets = [(p - 1, 0, smalls[p][29:30, 0:LANES]) for p in range(3)]
    nets += [(p - 1, q, far[p][29:30, 0:LANES]) for p in range(3)]
    put_coefs(coef_ref, rows, off_x, off_y, nets, smalls[1])
    spread(far, side_par)
    total_ref[...] = jnp.zeros((8, LANES), F32)
    for k, c in enumerate(range(3, len(layout))):
        own_step(
            total_ref, coef_ref, 1, c, par_ref, mid_ref[1, 0:H, :], k, s_ref, state_ref
        )
    for p in (0, 2):
        near_step(total_ref, coef_ref, p, 3, par_ref, p, mid_ref[p, 0:H, :])
    for p, c in ((0, 0), (1, 0), (1, 1), (2, 1), (1, 2)):
        near_step(total_ref, coef_ref, 3 + p, c, side_par, p, side_ref[p, 0:H, :])
    return area, rows[6]


def high_kernel(
    mid_ref, hi_ref, par_ref, coef_ref, info_ref, s_ref, state_ref, side_par, chunk_ref, total_ref
):
    work = (coef_ref, total_ref, side_par, chunk_ref, s_ref, state_ref)
    area, source = side(HIGH, 1, mid_ref, hi_ref, None, par_ref, work)
    info_ref[0] = total_ref[...]
    info_ref[1] = area
    info_ref[2] = source


def moved(total, layout):
    places = {}
    for c, regions in enumerate(layout[:3]):
        for k, region in enumerate(regions):
            places[region] = (c, SPAN * k)
    rows = []
    for regions in WINDOW:
        parts = []
        for region in regions:
            if region in places:
                c, at = places[region]
                parts.append(total[c : c + 1, at : at + SPAN])
            else:
                parts.append(jnp.zeros((1, SPAN), F32))
        parts += [jnp.zeros((1, SPAN), F32)] * (4 - len(parts))
        rows.append(jnp.concatenate(parts, axis=1))
    return jnp.concatenate(rows + [jnp.zeros((1, LANES), F32)], axis=0)


def last_kernel(
    mid_ref,
    lo_ref,
    hi_ref,
    w_ref,
    par_ref,
    coef_m,
    info_m,
    s_m,
    state_m,
    coef_h,
    info_h,
    s_h,
    state_h,
    gw_ref,
    gs_ref,
    stat_ref,
    coef_l,
    s_l,
    state_l,
    side_par,
    chunk_ref,
    total_ref,
    d_ref,
    acc_ref,
):
    work = (coef_l, total_ref, side_par, chunk_ref, s_l, state_l)
    area_l, source_l = side(BELOW, -1, mid_ref, lo_ref, hi_ref, par_ref, work)
    below = total_ref[...]
    high = info_h[0]

    def joined(m, h, l):
        return jnp.concatenate(
            [m[0:4], h[3:4], l[3:5], jnp.zeros((1, LANES), F32)], axis=0
        )

    area = joined(info_m[1], info_h[1], area_l)
    source = joined(info_m[2], info_h[2], source_l)
    total = joined(info_m[0], high, below) + moved(high, HIGH) + moved(below, BELOW)
    residual = total - source
    line = lax.broadcasted_iota(jnp.int32, (8, LANES), 0)
    own = jnp.where(line < 4, info_m[3], 0.0)
    loss = jnp.sum(own * area * residual * residual)
    total_ref[...] = 2.0 * area * residual
    w1, w2, pw = par_ref.at[1, 0], par_ref.at[1, 1], par_ref.at[1, 5]
    places = [(coef_m, c, s_m, state_m, c) for c in range(4)]
    places += [(coef_h, 3, s_h, state_h, 0), (coef_l, 3, s_l, state_l, 0)]
    places += [(coef_l, 4, s_l, state_l, 1)]

    def put(ref, parts, first):
        value = functools.reduce(lambda one, two: one + two, parts)
        ref[...] = value if first else ref[...] + value

    def cotangents(group, first):
        base, mix = [], []
        for row in group:
            coef_ref, c, _, state_ref, k = places[row]
            c3 = coef_ref[1, 5, c : c + 1, :]
            adjoint = total_ref[row : row + 1, :]
            scale = state_ref[k, 2] * adjoint
            d_base = scale * state_ref[k, 3]
            base.append(d_base)
            mix.append(state_ref[k, 1] * adjoint)
            d_ref[row, :, 0:LANES] = d_base.astype(BF16)
            d_ref[row, :, LANES : 2 * LANES] = (scale * state_ref[k, 4]).astype(BF16)
            d_ref[row, :, 2 * LANES : 3 * LANES] = (scale * state_ref[k, 5]).astype(BF16)
            d_ref[row, :, 3 * LANES :] = (scale * c3).astype(BF16)
        put(acc_ref.at[4], base, first)
        put(acc_ref.at[5], mix, first)

    groups = ((0, 1), (2, 3), (4, 5), (6,))
    cotangents(groups[0], True)
    for g, group in enumerate(groups):
        d_streams = [
            jnp.dot(w_ref[0, 0], d_ref[row], preferred_element_type=F32) for row in group
        ]
        terms = [
            lax.dot_general(
                places[row][2][places[row][4]],
                d_ref[row],
                (((1,), (1,)), ((), ())),
                preferred_element_type=F32,
            )
            for row in group
        ]
        if g + 1 < len(groups):
            cotangents(groups[g + 1], False)
        put(gw_ref, terms, g == 0)
        parts = [[], [], [], []]
        for row, ds in zip(group, d_streams):
            coef_ref, c, _, state_ref, k = places[row]
            xi, eta = coef_ref[1, 0, c : c + 1, :], coef_ref[1, 1, c : c + 1, :]
            h1 = state_ref[k, 0]
            ds0, ds1 = ds[:, 0:LANES], ds[:, LANES : 2 * LANES]
            ds2, ds3 = ds[:, 2 * LANES : 3 * LANES], ds[:, 3 * LANES :]
            d1 = 1.0 - h1 * h1
            cross = w1[...] * ds1 + w2[...] * ds2
            d_pre = d1 * (ds0 + pw[...] * ds3 * (3.0 * d1 - 2.0) - (4.0 * h1) * cross)
            d1x2 = 2.0 * d1
            parts[0].append(d1x2 * ds1 + xi * d_pre)
            parts[1].append(d1x2 * ds2 + eta * d_pre)
            parts[2].append(d_pre)
            parts[3].append(h1 * d1 * ds3)
        for k, part in enumerate(parts):
            put(acc_ref.at[k], part, g == 0)
    sums = [jnp.sum(acc_ref[k], axis=1, keepdims=True) for k in range(6)]
    turn = -16.0 * sums[3]
    grid = jnp.concatenate(
        [
            sums[0] + turn * w1[:, 0:1],
            sums[1] + turn * w2[:, 0:1],
            sums[2],
            sums[4],
            sums[5],
            jnp.zeros((H, 3), F32),
        ],
        axis=1,
    )
    gs = jnp.transpose(grid)
    gs_ref[...] = gs
    gw = gw_ref[...]
    square = jnp.sum(gw * gw) + jnp.sum(gs * gs)
    lane = lax.broadcasted_iota(jnp.int32, stat_ref.shape, 2)
    stat_ref[...] = jnp.where(lane == 0, square, jnp.where(lane == 1, loss, 0.0))


def sum_kernel(got_ref, out_ref):
    total = jnp.sum(got_ref[...], axis=0, keepdims=True)
    out_ref[...] = jnp.broadcast_to(total, out_ref.shape)


def scale_kernel(nets, got_ref, gw_ref, gs_ref, o0, o1, o2, o3, o4, loss_ref):
    total = jnp.sum(got_ref[...], axis=0)
    rms = jnp.sqrt(total[:, 0:1] / (nets * (H * H + 5 * H)) + EPS)
    gs = gs_ref[...] / rms
    o0[0, 0] = gs[0:2]
    o1[0] = gs[2:3]
    o2[0, 0] = gw_ref[...] / rms
    o3[0] = gs[3:4]
    o4[0] = gs[4:5]
    loss_ref[...] = total[:, 1:2]


def call(kernel, outs, scratch=(), limit=16 << 20, flops=0, place=pltpu.VMEM):
    extra = {}
    if place != pltpu.VMEM:
        extra["in_specs"] = [pl.BlockSpec(memory_space=place)] * 10
    return pl.pallas_call(
        kernel,
        out_shape=outs,
        scratch_shapes=scratch,
        compiler_params=pltpu.CompilerParams(vmem_limit_bytes=limit),
        cost_estimate=pl.CostEstimate(
            flops=flops, bytes_accessed=1 << 18, transcendentals=0
        ),
        **extra,
    )


def shape(dims, kind=F32):
    return jax.ShapeDtypeStruct(dims, kind)


GX = ("z", "yh", "c")
GY = ("yl", "x")
FIRST = ("z", "c")
SECOND = ("yh", "yl", "x")


def local(
    points,
    diffusion,
    drift,
    ionization,
    source,
    in_weight,
    in_bias,
    mid_weight,
    mid_bias,
    out_weight,
):
    count_x = lax.axis_size(GX)
    count_y = lax.axis_size(GY)
    inputs = (
        points.transpose(1, 2, 0, 3),
        diffusion,
        drift.transpose(1, 2, 0, 3),
        ionization,
        source,
        in_weight,
        in_bias,
        mid_weight,
        mid_bias,
        out_weight,
    )
    payload, table = call(
        pack_kernel,
        (shape((ROWS, H), BF16), shape((8, 384))),
        tuple(pltpu.VMEM(x.shape, x.dtype) for x in inputs)
        + (pltpu.SemaphoreType.DMA((13,)),),
        place=pl.ANY,
        limit=16 << 20,
    )(*(pltpu.with_memory_space_constraint(x, pltpu.HBM) for x in inputs))
    forth = [(i, i + 1) for i in range(count_x - 1)]
    after = lax.ppermute(payload, GX, [(j, i) for i, j in forth])
    before = lax.ppermute(payload, GX, forth)
    row = jnp.stack([before, payload, after])
    pairs = [(i, i ^ 1) for i in range(count_y)]
    bonds = [(i, (i + 1) % count_y) for i in range(1, count_y, 2)]
    above = lax.ppermute(row, GY, pairs)
    below = lax.ppermute(row, GY, bonds + [(j, i) for i, j in bonds])
    first = lax.axis_size(FIRST)
    second = lax.axis_size(SECOND)

    def kept(chunks):
        return ((chunks, H, 4 * LANES), BF16), ((chunks, 6, H, LANES), F32)

    def outs(nets, infos, chunks):
        return (shape((nets, 6, 8, LANES)), shape((infos, 8, LANES))) + tuple(
            shape(*k) for k in kept(chunks)
        )

    chunk = pltpu.VMEM((8, 8, LANES), F32)
    total = pltpu.VMEM((8, LANES), F32)
    spreads = (3, 6, H, LANES)
    params, *middle = call(
        middle_kernel, (shape(spreads),) + outs(3, 4, 4), (chunk, total), flops=10**9
    )(row, table)
    high = call(
        high_kernel,
        outs(6, 3, 1),
        (pltpu.VMEM(spreads, F32), chunk, total),
        flops=10**9,
    )(row, above, params)
    grad_w, grad_s, stat = call(
        last_kernel,
        (shape((H, H)), shape((8, H)), shape((first, 1, LANES))),
        (
            pltpu.VMEM((6, 6, 8, LANES), F32),
            *(pltpu.VMEM(*k) for k in kept(2)),
            pltpu.VMEM(spreads, F32),
            chunk,
            total,
            pltpu.VMEM((7, H, 4 * LANES), BF16),
            pltpu.VMEM((6, H, LANES), F32),
        ),
        limit=24 << 20,
        flops=10**9,
    )(row, below, above, mid_weight, params, *middle, *high)
    got = lax.all_to_all(stat, FIRST, 0, 0, tiled=True)
    part = call(sum_kernel, shape((second, 1, LANES)))(got)
    got = lax.all_to_all(part, SECOND, 0, 0, tiled=True)
    outs = call(
        lambda *refs: scale_kernel(count_x * count_y, *refs),
        (
            shape((1, 1, 2, H)),
            shape((1, 1, H)),
            shape((1, 1, H, H)),
            shape((1, 1, H)),
            shape((1, 1, H)),
            shape((1, 1)),
        ),
    )(got, grad_w, grad_s)
    return (*outs[:5], outs[5].reshape(()))


def solution(mesh):
    fine = Mesh(
        mesh.devices.reshape(8, 2, 2, 4, 4), ("z", "yh", "c", "yl", "x")
    )
    return jax.shard_map(
        local,
        mesh=fine,
        in_specs=(
            P(None, GX, GY, None),
            P(GX, GY, None),
            P(None, GX, GY, None),
            P(GX, GY, None),
            P(GX, GY, None),
            P(GX, GY, None, None),
            P(GX, GY, None),
            P(GX, GY, None, None),
            P(GX, GY, None),
            P(GX, GY, None),
        ),
        out_specs=(
            P(GX, GY, None, None),
            P(GX, GY, None),
            P(GX, GY, None, None),
            P(GX, GY, None),
            P(GX, GY, None),
            P(),
        ),
        check_vma=False,
    )
```

```python
import functools

import jax
import jax.numpy as jnp
from jax import lax
from jax.experimental import pallas as pl
from jax.experimental.pallas import tpu as pltpu
from jax.sharding import Mesh, PartitionSpec as P

DELTA = 0.25
EPS = 1e-06
H = 256
LANES = 128
SPAN = 32
ROWS = 288
F32 = jnp.float32
BF16 = jnp.bfloat16

MIDDLE = (
    ((0, 2), (1, 2), (3, 2), (4, 2)),
    ((0, 3), (1, 3), (3, 3), (4, 3)),
    ((0, 1), (1, 1), (3, 1), (4, 1)),
)
HIGH = (
    ((0, 3), (0, 4), (1, 3), (1, 4)),
    ((3, 3), (3, 4), (4, 3), (4, 4)),
    ((2, 3), (2, 4)),
    ((0, 4), (1, 4), (3, 4), (4, 4)),
    ((2, 2), (2, 3), (2, 4)),
)
BELOW = (
    ((0, 0), (0, 1), (1, 0), (1, 1)),
    ((3, 0), (3, 1), (4, 0), (4, 1)),
    ((2, 0), (2, 1)),
    ((0, 0), (1, 0), (3, 0), (4, 0)),
    ((2, 0), (2, 1)),
)
EARLY = (MIDDLE[0], MIDDLE[1], HIGH[3], HIGH[4])
LATE = (MIDDLE[2], BELOW[3], BELOW[4])
PLACE = {
    (0, 0): 0,
    (0, 1): 32,
    (0, 2): 64,
    (1, 0): 96,
    (2, 0): 128,
    (2, 1): 160,
    (2, 2): 192,
    (1, 2): 224,
    (1, 1): 256,
}
LOW = (0.0, DELTA, 1.0 - DELTA)
WIDTH = (DELTA, 1.0 - 2.0 * DELTA, DELTA)


def smooth_rise(coord):
    ramp = jnp.clip((coord + DELTA) / (2.0 * DELTA), 0.0, 1.0)
    value = ramp * ramp * ramp * (10.0 - 15.0 * ramp + 6.0 * ramp * ramp)
    slope = 30.0 * ramp * ramp * (1.0 - ramp) * (1.0 - ramp) / (2.0 * DELTA)
    bend = 60.0 * ramp * (1.0 - ramp) * (1.0 - 2.0 * ramp) / (4.0 * DELTA * DELTA)
    return (value, slope, bend)


def bump(coord):
    rise_a = smooth_rise(coord)
    rise_b = smooth_rise(coord - 1.0)
    return (rise_a[0] - rise_b[0], rise_a[1] - rise_b[1], rise_a[2] - rise_b[2])


def pack_kernel(*refs):
    sources, (pay_ref, tab_ref), buffers, sems = (
        refs[:10],
        refs[10:12],
        refs[12:22],
        refs[22],
    )
    pts, dif, dri, ion, src, w_in, b_in, w_mid, b_mid, w_out = buffers
    strips = [pl.ds(64 * k, 64) for k in range(4)]
    pairs = [(sources[7].at[0, 0, k], w_mid.at[0, 0, k]) for k in strips]
    pairs += [(sources[k], buffers[k]) for k in range(10) if k != 7]
    copies = [
        pltpu.make_async_copy(one, two, sems.at[k]) for k, (one, two) in enumerate(pairs)
    ]
    for copy in copies:
        copy.start()
    for copy in copies[4:]:
        copy.wait()
    zeros = jnp.zeros((1, SPAN), F32)
    ones = jnp.ones((1, SPAN), F32)
    pieces = {}
    for a in range(3):
        for b in range(3):
            rows = [
                LOW[a] + WIDTH[a] * pts[a, b, 0:1, :],
                LOW[b] + WIDTH[b] * pts[a, b, 1:2, :],
                dif[a, b : b + 1, :],
                dri[a, b, 0:1, :],
                dri[a, b, 1:2, :],
                ion[a, b : b + 1, :],
                src[a, b : b + 1, :],
                ones,
            ]
            pieces[a, b] = jnp.concatenate(rows, axis=0)
    blank = jnp.concatenate([zeros] * 8, axis=0)
    turn = lax.rem(lax.axis_index("x"), 2) == 1
    placed = {
        at: jnp.where(turn, pieces[a, 2 - b], pieces[a, b]) for (a, b), at in PLACE.items()
    }
    order = [placed.get(32 * k, blank) for k in range(12)]
    tabs = [jnp.concatenate(order[4 * k : 4 * k + 4], axis=1) for k in range(3)]
    for k in range(3):
        tab_ref[:, 128 * k : 128 * k + 128] = tabs[k]
    edge = jnp.concatenate(tabs[:2], axis=1)
    high = edge.astype(BF16).astype(F32)
    rest = edge - high
    mid = rest.astype(BF16).astype(F32)
    low = rest - mid
    small = jnp.concatenate(
        [
            w_in[0, 0].astype(F32),
            b_in[0].astype(F32),
            b_mid[0].astype(F32),
            w_out[0].astype(F32),
            jnp.ones((1, H), F32),
            jnp.where(turn, -1.0, 1.0) * jnp.ones((1, H), F32),
            jnp.zeros((1, H), F32),
        ],
        axis=0,
    )
    pay_ref[H:ROWS, :] = jnp.concatenate([high, mid, low, small], axis=0).astype(BF16)
    for copy in copies[:4]:
        copy.wait()
    pay_ref[0:H, :] = jnp.transpose(w_mid[0, 0].astype(F32)).astype(BF16)


def small_rows(ref):
    return [ref[2 - p, H:ROWS, :].astype(F32) for p in range(3)]


def tables(smalls):
    return [(s[0:8] + s[8:16]) + s[16:24] for s in smalls]


def gather_rows(chunk_ref, layout, points):
    blank = jnp.zeros((8, SPAN), F32)
    for c, regions in enumerate(layout):
        parts = []
        for big_a, big_b in regions:
            p = 0 if big_a == 0 else 2 if big_a == 4 else 1
            q = 0 if big_b == 0 else 2 if big_b == 4 else 1
            at = PLACE[(2, big_a - 1, 0)[p], (0, big_b - 1, 2)[q]]
            parts.append(points[q][p][:, at : at + SPAN])
        parts += [blank] * (4 - len(parts))
        chunk_ref[c] = jnp.concatenate(parts, axis=1)
    for c in range(len(layout), 8):
        chunk_ref[c] = jnp.zeros((8, LANES), F32)
    return [chunk_ref[:, k, :] for k in range(8)]


def frame(layout, flag):
    spot = lax.broadcasted_iota(jnp.int32, (8, LANES), 0) * 4 + (
        lax.broadcasted_iota(jnp.int32, (8, LANES), 1) // SPAN
    )

    def among(test):
        hit = jnp.zeros((8, LANES), F32)
        for c, regions in enumerate(layout):
            for k, region in enumerate(regions):
                if test(region):
                    hit = jnp.where(spot == 4 * c + k, 1.0, hit)
        return hit

    off_x = among(lambda r: r[0] == 4) - among(lambda r: r[0] == 0)
    off_y = among(lambda r: r[1] == 4) - among(lambda r: r[1] == 0)
    own = (1.0 - off_x * off_x) * (1.0 - off_y * off_y)
    wide_x = DELTA + (1.0 - 3.0 * DELTA) * among(lambda r: r[0] == 2)
    wide_y = DELTA + (1.0 - 3.0 * DELTA) * among(lambda r: r[1] == 2)
    return off_x, off_y, wide_x * wide_y / SPAN * flag, own


def put_coefs(coef_ref, rows, off_x, off_y, nets, small):
    pos_x, pos_y, diff, vel_x, vel_y, rate = rows[:6]
    way = small[30:31, 0:LANES]
    coords_x = {p: pos_x + (off_x - float(p)) for p, _, _ in nets}
    coords_y = {q: pos_y + way * (off_y - float(q)) for _, q, _ in nets}
    bumps_x = {p: bump(t) for p, t in coords_x.items()}
    bumps_y = {q: bump(s) for q, s in coords_y.items()}
    for n, (p, q, present) in enumerate(nets):
        b_x, b_y = bumps_x[p], bumps_y[q]
        window = b_x[0] * b_y[0] * present
        window_x = b_x[1] * b_y[0] * present
        window_y = b_x[0] * b_y[1] * present
        window_l = (b_x[2] * b_y[0] + b_x[0] * b_y[2]) * present
        coef_ref[n, 0] = 2.0 * coords_x[p] - 1.0
        coef_ref[n, 1] = 2.0 * coords_y[q] - 1.0
        coef_ref[n, 2] = (
            -diff * window_l + vel_x * window_x + vel_y * window_y - rate * window
        )
        coef_ref[n, 3] = -2.0 * diff * window_x + vel_x * window
        coef_ref[n, 4] = -2.0 * diff * window_y + vel_y * window
        coef_ref[n, 5] = -diff * window
    left = lax.broadcasted_iota(jnp.int32, (8, LANES), 1) < LANES // 2
    for k in range(6):
        coef_ref[len(nets), k] = jnp.where(left, coef_ref[0, k], coef_ref[2, k])


def spread(smalls, par_ref):
    lane = lax.broadcasted_iota(jnp.int32, (8, 5 * LANES), 1) // LANES
    line = lax.broadcasted_iota(jnp.int32, (8, 5 * LANES), 0)
    pick = jnp.where(lane == line, 1.0, 0.0).astype(BF16)
    for n, small in enumerate(smalls):
        wide = lax.dot_general(
            small[24:32].astype(BF16),
            pick,
            (((0,), (0,)), ((), ())),
            preferred_element_type=F32,
        )
        for k in range(5):
            par_ref[n, k] = wide[:, LANES * k : LANES * k + LANES]
        w_first, w_second = wide[:, 0:LANES], wide[:, LANES : 2 * LANES]
        par_ref[n, 5] = -8.0 * (w_first * w_first + w_second * w_second)


def forward(par_ref, n, weights, xi, eta):
    w_first, w_second = par_ref[n, 0], par_ref[n, 1]
    h1 = jnp.tanh(xi * w_first + eta * w_second + par_ref[n, 2])
    d1 = 1.0 - h1 * h1
    d1x2 = 2.0 * d1
    streams = jnp.concatenate(
        [
            h1.astype(BF16),
            (d1x2 * w_first).astype(BF16),
            (d1x2 * w_second).astype(BF16),
            (h1 * d1 * par_ref[n, 5]).astype(BF16),
        ],
        axis=1,
    )
    mixed = [jnp.dot(w, streams, preferred_element_type=F32) for w in weights]
    if len(mixed) == 2:
        lane = lax.broadcasted_iota(jnp.int32, (1, 4 * LANES), 1)
        mixed = [jnp.where(lane % LANES < LANES // 2, *mixed)]
    mixed = mixed[0]
    h2 = jnp.tanh(mixed[:, 0:LANES] + par_ref[n, 3])
    gx = mixed[:, LANES : 2 * LANES]
    gy = mixed[:, 2 * LANES : 3 * LANES]
    curve = mixed[:, 3 * LANES :]
    return h1, streams, h2, gx, gy, curve


def coefs(coef_ref, n, c):
    return [coef_ref[n, k, c : c + 1, :] for k in range(6)]


def add_field(total_ref, c, mix, head):
    total_ref[c : c + 1, :] += jnp.sum(mix * head, axis=0, keepdims=True)


def near_step(total_ref, coef_ref, n, c, par_ref, m, weights):
    xi, eta, c0, c1, c2, c3 = coefs(coef_ref, n, c)
    _, _, h2, gx, gy, curve = forward(par_ref, m, weights, xi, eta)
    d2 = 1.0 - h2 * h2
    square = gx * gx + gy * gy
    inner = c1 * gx + c2 * gy + c3 * (curve - 2.0 * h2 * square)
    add_field(total_ref, c, c0 * h2 + d2 * inner, par_ref[m, 4])


def own_step(total_ref, coef_ref, n, c, par_ref, weights, k, s_ref, state_ref):
    xi, eta, c0, c1, c2, c3 = coefs(coef_ref, n, c)
    h1, streams, h2, gx, gy, curve = forward(par_ref, 1, weights, xi, eta)
    d2 = 1.0 - h2 * h2
    square = gx * gx + gy * gy
    inner = c1 * gx + c2 * gy + c3 * (curve - 2.0 * h2 * square)
    mix = c0 * h2 + d2 * inner
    head = par_ref[1, 4]
    add_field(total_ref, c, mix, head)
    turn = (4.0 * c3) * h2
    s_ref[k] = streams
    state_ref[k, 0] = h1
    state_ref[k, 1] = mix
    state_ref[k, 2] = head * d2
    state_ref[k, 3] = c0 - 2.0 * (d2 * square * c3 + h2 * inner)
    state_ref[k, 4] = c1 - turn * gx
    state_ref[k, 5] = c2 - turn * gy


def middle_kernel(
    mid_ref, tab_ref, par_ref, coef_ref, info_ref, s_ref, state_ref, chunk_ref, total_ref
):
    smalls = small_rows(mid_ref)
    points = tables(smalls)
    points[1] = tab_ref[...]
    rows = gather_rows(chunk_ref, MIDDLE, [None, points, None])
    off_x, off_y, area, own = frame(MIDDLE, rows[7])
    nets = [(p - 1, 0, smalls[p][29:30, 0:LANES]) for p in range(3)]
    put_coefs(coef_ref, rows, off_x, off_y, nets, smalls[1])
    spread(smalls, par_ref)
    left = lax.broadcasted_iota(jnp.int32, (H, LANES), 1) < LANES // 2
    for k in range(6):
        par_ref[3, k] = jnp.where(left, par_ref[0, k], par_ref[2, k])
    total_ref[...] = jnp.zeros((8, LANES), F32)
    weights = [mid_ref[2 - p, 0:H, :] for p in range(3)]
    for c in range(3):
        own_step(total_ref, coef_ref, 1, c, par_ref, weights[1:2], c, s_ref, state_ref)
    for c in range(3):
        near_step(total_ref, coef_ref, 3, c, par_ref, 3, weights[0::2])
    info_ref[0] = total_ref[...]
    info_ref[1] = area
    info_ref[2] = rows[6]
    info_ref[3] = own


def side(layout, q, mid_ref, side_ref, own_table, par_ref, work):
    coef_ref, total_ref, side_par, chunk_ref, s_ref, state_ref = work
    smalls = small_rows(mid_ref)
    far = small_rows(side_ref)
    points = [None, tables(smalls), None]
    if own_table is not None:
        points[1][1] = own_table
    points[1 + q] = tables(far)
    rows = gather_rows(chunk_ref, layout, points)
    off_x, off_y, area, own = frame(layout, rows[7])
    nets = [(p - 1, 0, smalls[p][29:30, 0:LANES]) for p in range(3)]
    nets += [(p - 1, q, far[p][29:30, 0:LANES]) for p in range(3)]
    put_coefs(coef_ref, rows, off_x, off_y, nets, smalls[1])
    spread(far, side_par)
    total_ref[...] = jnp.zeros((8, LANES), F32)
    weights = [mid_ref[2 - p, 0:H, :] for p in range(3)]
    for k in range(2):
        own_step(
            total_ref, coef_ref, 1, 3 + k, par_ref, weights[1:2], k, s_ref, state_ref
        )
    near_step(total_ref, coef_ref, 6, 3, par_ref, 3, weights[0::2])
    for p, c in ((0, 0), (1, 0), (1, 1), (2, 1), (1, 2)):
        near_step(total_ref, coef_ref, 3 + p, c, side_par, p, [side_ref[2 - p, 0:H, :]])
    return area, rows[6], own


def moved(total, layout, target):
    places = {}
    for c, regions in enumerate(layout[:3]):
        for k, region in enumerate(regions):
            places[region] = (c, SPAN * k)
    rows = []
    for regions in target:
        parts = []
        for region in regions:
            if region in places:
                c, at = places[region]
                parts.append(total[c : c + 1, at : at + SPAN])
            else:
                parts.append(jnp.zeros((1, SPAN), F32))
        parts += [jnp.zeros((1, SPAN), F32)] * (4 - len(parts))
        rows.append(jnp.concatenate(parts, axis=1))
    return jnp.concatenate(rows + [jnp.zeros((8 - len(rows), LANES), F32)], axis=0)


def joined(one, first, last, two):
    blank = jnp.zeros((6 - (last - first), LANES), F32)
    return jnp.concatenate([one[first:last], two[3:5], blank], axis=0)


def residuals(info_m, first, last, here, total_ref, layout, target):
    area_s, source_s, own_s = here
    totals = total_ref[...]
    area = joined(info_m[1], first, last, area_s)
    source = joined(info_m[2], first, last, source_s)
    own = joined(info_m[3], first, last, own_s)
    total = joined(info_m[0], first, last, totals) + moved(totals, layout, target)
    residual = total - source
    total_ref[...] = 2.0 * area * residual
    return own * area * residual * residual


def put(ref, parts, base):
    value = functools.reduce(lambda one, two: one + two, parts)
    ref[...] = value if base is None else base[...] + value


def backward(places, groups, total_ref, par_ref, w_ref, d_ref, acc_ref, gw_ref, base):
    w1, w2, pw = par_ref.at[1, 0], par_ref.at[1, 1], par_ref.at[1, 5]

    def start(k, g):
        return acc_ref.at[k] if g else None if base is None else base[0].at[k]

    def cotangents(g):
        d_bases, mixes = [], []
        for row in groups[g]:
            coef_ref, c, _, state_ref, k = places[row]
            c3 = coef_ref[1, 5, c : c + 1, :]
            adjoint = total_ref[row : row + 1, :]
            scale = state_ref[k, 2] * adjoint
            d_base = scale * state_ref[k, 3]
            d_bases.append(d_base)
            mixes.append(state_ref[k, 1] * adjoint)
            d_ref[row, :, 0:LANES] = d_base.astype(BF16)
            d_ref[row, :, LANES : 2 * LANES] = (scale * state_ref[k, 4]).astype(BF16)
            d_ref[row, :, 2 * LANES : 3 * LANES] = (scale * state_ref[k, 5]).astype(BF16)
            d_ref[row, :, 3 * LANES :] = (scale * c3).astype(BF16)
        put(acc_ref.at[4], d_bases, start(4, g))
        put(acc_ref.at[5], mixes, start(5, g))

    cotangents(0)
    for g, group in enumerate(groups):
        d_streams = [
            jnp.dot(w_ref[0, 0], d_ref[row], preferred_element_type=F32) for row in group
        ]
        terms = [
            lax.dot_general(
                places[row][2][places[row][4]],
                d_ref[row],
                (((1,), (1,)), ((), ())),
                preferred_element_type=F32,
            )
            for row in group
        ]
        if g + 1 < len(groups):
            cotangents(g + 1)
        put(gw_ref, terms, gw_ref if g else None if base is None else base[1])
        parts = [[], [], [], []]
        for row, ds in zip(group, d_streams):
            coef_ref, c, _, state_ref, k = places[row]
            xi, eta = coef_ref[1, 0, c : c + 1, :], coef_ref[1, 1, c : c + 1, :]
            h1 = state_ref[k, 0]
            ds0, ds1 = ds[:, 0:LANES], ds[:, LANES : 2 * LANES]
            ds2, ds3 = ds[:, 2 * LANES : 3 * LANES], ds[:, 3 * LANES :]
            d1 = 1.0 - h1 * h1
            cross = w1[...] * ds1 + w2[...] * ds2
            d_pre = d1 * (ds0 + pw[...] * ds3 * (3.0 * d1 - 2.0) - (4.0 * h1) * cross)
            d1x2 = 2.0 * d1
            parts[0].append(d1x2 * ds1 + xi * d_pre)
            parts[1].append(d1x2 * ds2 + eta * d_pre)
            parts[2].append(d_pre)
            parts[3].append(h1 * d1 * ds3)
        for k, part in enumerate(parts):
            put(acc_ref.at[k], part, start(k, g))


def high_kernel(
    mid_ref,
    hi_ref,
    tab_ref,
    w_ref,
    par_ref,
    coef_m,
    info_m,
    s_m,
    state_m,
    acc_ref,
    gw_ref,
    loss_ref,
    coef_ref,
    s_ref,
    state_ref,
    side_par,
    chunk_ref,
    total_ref,
    d_ref,
):
    work = (coef_ref, total_ref, side_par, chunk_ref, s_ref, state_ref)
    here = side(HIGH, 1, mid_ref, hi_ref, tab_ref[...], par_ref, work)
    loss_ref[...] = residuals(info_m, 0, 2, here, total_ref, HIGH, EARLY)
    places = [(coef_m, c, s_m, state_m, c) for c in range(2)]
    places += [(coef_ref, 3 + k, s_ref, state_ref, k) for k in range(2)]
    backward(
        places, ((0, 1), (2, 3)), total_ref, par_ref, w_ref, d_ref, acc_ref, gw_ref, None
    )


def last_kernel(
    mid_ref,
    lo_ref,
    w_ref,
    par_ref,
    coef_m,
    info_m,
    s_m,
    state_m,
    acc_h,
    gw_h,
    loss_h,
    gw_ref,
    gs_ref,
    stat_ref,
    coef_ref,
    s_ref,
    state_ref,
    side_par,
    chunk_ref,
    total_ref,
    d_ref,
    acc_ref,
):
    work = (coef_ref, total_ref, side_par, chunk_ref, s_ref, state_ref)
    here = side(BELOW, -1, mid_ref, lo_ref, None, par_ref, work)
    loss = jnp.sum(
        loss_h[...] + residuals(info_m, 2, 3, here, total_ref, BELOW, LATE)
    )
    places = [(coef_m, 2, s_m, state_m, 2)]
    places += [(coef_ref, 3 + k, s_ref, state_ref, k) for k in range(2)]
    base = (acc_h, gw_h)
    backward(
        places, ((0, 1), (2,)), total_ref, par_ref, w_ref, d_ref, acc_ref, gw_ref, base
    )
    sums = [jnp.sum(acc_ref[k], axis=1, keepdims=True) for k in range(6)]
    turn = -16.0 * sums[3]
    grid = jnp.concatenate(
        [
            sums[0] + turn * par_ref[1, 0, :, 0:1],
            sums[1] + turn * par_ref[1, 1, :, 0:1],
            sums[2],
            sums[4],
            sums[5],
            jnp.zeros((H, 3), F32),
        ],
        axis=1,
    )
    gs_ref[...] = jnp.transpose(grid)
    gw = gw_ref[...]
    square = jnp.sum(gw * gw) + jnp.sum(grid * grid)
    lane = lax.broadcasted_iota(jnp.int32, stat_ref.shape, 2)
    stat_ref[...] = jnp.where(lane == 0, square, jnp.where(lane == 1, loss, 0.0))


def sum_kernel(got_ref, out_ref):
    total = jnp.sum(got_ref[...], axis=0, keepdims=True)
    out_ref[...] = jnp.broadcast_to(total, out_ref.shape)


def scale_kernel(nets, got_ref, gw_ref, gs_ref, o0, o1, o2, o3, o4, loss_ref):
    total = jnp.sum(got_ref[...], axis=0)
    rms = jnp.sqrt(total[:, 0:1] / (nets * (H * H + 5 * H)) + EPS)
    gs = gs_ref[...] / rms
    o0[0, 0] = gs[0:2]
    o1[0] = gs[2:3]
    o2[0, 0] = gw_ref[...] / rms
    o3[0] = gs[3:4]
    o4[0] = gs[4:5]
    loss_ref[...] = total[:, 1:2]


def call(kernel, outs, scratch=(), limit=16 << 20, flops=0, place=pltpu.VMEM):
    extra = {}
    if place != pltpu.VMEM:
        extra["in_specs"] = [pl.BlockSpec(memory_space=place)] * 10
    return pl.pallas_call(
        kernel,
        out_shape=outs,
        scratch_shapes=scratch,
        compiler_params=pltpu.CompilerParams(vmem_limit_bytes=limit),
        cost_estimate=pl.CostEstimate(
            flops=flops, bytes_accessed=1 << 18, transcendentals=0
        ),
        **extra,
    )


def shape(dims, kind=F32):
    return jax.ShapeDtypeStruct(dims, kind)


GX = ("z", "yh", "c")
GY = ("yl", "x")
FIRST = ("z", "c")
SECOND = ("yh", "yl", "x")


def local(
    points,
    diffusion,
    drift,
    ionization,
    source,
    in_weight,
    in_bias,
    mid_weight,
    mid_bias,
    out_weight,
):
    count_x = lax.axis_size(GX)
    count_y = lax.axis_size(GY)
    inputs = (
        points.transpose(1, 2, 0, 3),
        diffusion,
        drift.transpose(1, 2, 0, 3),
        ionization,
        source,
        in_weight,
        in_bias,
        mid_weight,
        mid_bias,
        out_weight,
    )
    payload, table = call(
        pack_kernel,
        (shape((ROWS, H), BF16), shape((8, 384))),
        tuple(pltpu.VMEM(x.shape, x.dtype) for x in inputs)
        + (pltpu.SemaphoreType.DMA((13,)),),
        place=pl.ANY,
        limit=16 << 20,
    )(*(pltpu.with_memory_space_constraint(x, pltpu.HBM) for x in inputs))
    forth = [(i, i + 1) for i in range(count_x - 1)]
    after = lax.ppermute(payload, GX, [(j, i) for i, j in forth])
    before = lax.ppermute(payload, GX, forth)
    row = jnp.stack([after, payload, before])
    pairs = [(i, i ^ 1) for i in range(count_y)]
    bonds = [(i, (i + 1) % count_y) for i in range(1, count_y, 2)]
    above = lax.ppermute(row, GY, pairs)
    below = lax.ppermute(row, GY, bonds + [(j, i) for i, j in bonds])
    first = lax.axis_size(FIRST)
    second = lax.axis_size(SECOND)

    def kept(chunks):
        return ((chunks, H, 4 * LANES), BF16), ((chunks, 6, H, LANES), F32)

    chunk = pltpu.VMEM((8, 8, LANES), F32)
    total = pltpu.VMEM((8, LANES), F32)
    accs = (6, H, LANES)
    params, *middle = call(
        middle_kernel,
        (shape((4, 6, H, LANES)), shape((4, 6, 8, LANES)), shape((4, 8, LANES)))
        + tuple(shape(*k) for k in kept(3)),
        (chunk, total),
        flops=10**9,
    )(row, table)

    def scratch(chunks):
        return (
            pltpu.VMEM((7, 6, 8, LANES), F32),
            *(pltpu.VMEM(*k) for k in kept(2)),
            pltpu.VMEM((3, 6, H, LANES), F32),
            chunk,
            total,
            pltpu.VMEM((chunks, H, 4 * LANES), BF16),
        )

    high = call(
        high_kernel,
        (shape(accs), shape((H, H)), shape((8, LANES))),
        scratch(4),
        limit=20 << 20,
        flops=10**9,
    )(row, above, table, mid_weight, params, *middle)
    grad_w, grad_s, stat = call(
        last_kernel,
        (shape((H, H)), shape((8, H)), shape((first, 1, LANES))),
        scratch(3) + (pltpu.VMEM(accs, F32),),
        limit=20 << 20,
        flops=10**9,
    )(row, below, mid_weight, params, *middle, *high)
    got = lax.all_to_all(stat, FIRST, 0, 0, tiled=True)
    part = call(sum_kernel, shape((second, 1, LANES)))(got)
    got = lax.all_to_all(part, SECOND, 0, 0, tiled=True)
    outs = call(
        lambda *refs: scale_kernel(count_x * count_y, *refs),
        (
            shape((1, 1, 2, H)),
            shape((1, 1, H)),
            shape((1, 1, H, H)),
            shape((1, 1, H)),
            shape((1, 1, H)),
            shape((1, 1)),
        ),
    )(got, grad_w, grad_s)
    return (*outs[:5], outs[5].reshape(()))


def solution(mesh):
    fine = Mesh(
        mesh.devices.reshape(8, 2, 2, 4, 4), ("z", "yh", "c", "yl", "x")
    )
    return jax.shard_map(
        local,
        mesh=fine,
        in_specs=(
            P(None, GX, GY, None),
            P(GX, GY, None),
            P(None, GX, GY, None),
            P(GX, GY, None),
            P(GX, GY, None),
            P(GX, GY, None, None),
            P(GX, GY, None),
            P(GX, GY, None, None),
            P(GX, GY, None),
            P(GX, GY, None),
        ),
        out_specs=(
            P(GX, GY, None, None),
            P(GX, GY, None),
            P(GX, GY, None, None),
            P(GX, GY, None),
            P(GX, GY, None),
            P(),
        ),
        check_vma=False,
    )
```

```python
import functools

import jax
import jax.numpy as jnp
from jax import lax
from jax.experimental import pallas as pl
from jax.experimental.pallas import tpu as pltpu
from jax.sharding import Mesh, PartitionSpec as P

DELTA = 0.25
EPS = 1e-06
H = 256
LANES = 128
SPAN = 32
ROWS = 288
F32 = jnp.float32
BF16 = jnp.bfloat16

MIDDLE = (
    ((0, 2), (1, 2), (3, 2), (4, 2)),
    ((0, 3), (1, 3), (3, 3), (4, 3)),
    ((0, 1), (1, 1), (3, 1), (4, 1)),
)
HIGH = (
    ((0, 3), (0, 4), (1, 3), (1, 4)),
    ((3, 3), (3, 4), (4, 3), (4, 4)),
    ((2, 3), (2, 4)),
    ((0, 4), (1, 4), (3, 4), (4, 4)),
    ((2, 2), (2, 3), (2, 4)),
)
BELOW = (
    ((0, 0), (0, 1), (1, 0), (1, 1)),
    ((3, 0), (3, 1), (4, 0), (4, 1)),
    ((2, 0), (2, 1)),
    ((0, 0), (1, 0), (3, 0), (4, 0)),
    ((2, 0), (2, 1)),
)
EARLY = (MIDDLE[0], MIDDLE[1], HIGH[3], HIGH[4])
LATE = (MIDDLE[2], BELOW[3], BELOW[4])
PLACE = {
    (0, 0): 0,
    (0, 1): 32,
    (0, 2): 64,
    (1, 0): 96,
    (2, 0): 128,
    (2, 1): 160,
    (2, 2): 192,
    (1, 2): 224,
    (1, 1): 256,
}
LOW = (0.0, DELTA, 1.0 - DELTA)
WIDTH = (DELTA, 1.0 - 2.0 * DELTA, DELTA)


def smooth_rise(coord):
    ramp = jnp.clip((coord + DELTA) / (2.0 * DELTA), 0.0, 1.0)
    value = ramp * ramp * ramp * (10.0 - 15.0 * ramp + 6.0 * ramp * ramp)
    slope = 30.0 * ramp * ramp * (1.0 - ramp) * (1.0 - ramp) / (2.0 * DELTA)
    bend = 60.0 * ramp * (1.0 - ramp) * (1.0 - 2.0 * ramp) / (4.0 * DELTA * DELTA)
    return (value, slope, bend)


def bump(coord):
    rise_a = smooth_rise(coord)
    rise_b = smooth_rise(coord - 1.0)
    return (rise_a[0] - rise_b[0], rise_a[1] - rise_b[1], rise_a[2] - rise_b[2])


def pack_kernel(*refs):
    sources, (pay_ref, tab_ref), buffers, sems = (
        refs[:10],
        refs[10:12],
        refs[12:22],
        refs[22],
    )
    pts, dif, dri, ion, src, w_in, b_in, w_mid, b_mid, w_out = buffers
    strips = [pl.ds(64 * k, 64) for k in range(4)]
    pairs = [(sources[7].at[0, 0, k], w_mid.at[0, 0, k]) for k in strips]
    pairs += [(sources[k], buffers[k]) for k in range(10) if k != 7]
    copies = [
        pltpu.make_async_copy(one, two, sems.at[k]) for k, (one, two) in enumerate(pairs)
    ]
    for copy in copies:
        copy.start()
    for copy in copies[4:]:
        copy.wait()
    zeros = jnp.zeros((1, SPAN), F32)
    ones = jnp.ones((1, SPAN), F32)
    pieces = {}
    for a in range(3):
        for b in range(3):
            rows = [
                LOW[a] + WIDTH[a] * pts[a, b, 0:1, :],
                LOW[b] + WIDTH[b] * pts[a, b, 1:2, :],
                dif[a, b : b + 1, :],
                dri[a, b, 0:1, :],
                dri[a, b, 1:2, :],
                ion[a, b : b + 1, :],
                src[a, b : b + 1, :],
                ones,
            ]
            pieces[a, b] = jnp.concatenate(rows, axis=0)
    blank = jnp.concatenate([zeros] * 8, axis=0)
    turn = lax.rem(lax.axis_index("x"), 2) == 1
    placed = {
        at: jnp.where(turn, pieces[a, 2 - b], pieces[a, b]) for (a, b), at in PLACE.items()
    }
    order = [placed.get(32 * k, blank) for k in range(12)]
    tabs = [jnp.concatenate(order[4 * k : 4 * k + 4], axis=1) for k in range(3)]
    for k in range(3):
        tab_ref[:, 128 * k : 128 * k + 128] = tabs[k]
    edge = jnp.concatenate(tabs[:2], axis=1)
    high = edge.astype(BF16).astype(F32)
    rest = edge - high
    mid = rest.astype(BF16).astype(F32)
    low = rest - mid
    small = jnp.concatenate(
        [
            w_in[0, 0].astype(F32),
            b_in[0].astype(F32),
            b_mid[0].astype(F32),
            w_out[0].astype(F32),
            jnp.ones((1, H), F32),
            jnp.where(turn, -1.0, 1.0) * jnp.ones((1, H), F32),
            jnp.zeros((1, H), F32),
        ],
        axis=0,
    )
    pay_ref[H:ROWS, :] = jnp.concatenate([high, mid, low, small], axis=0).astype(BF16)
    for copy in copies[:4]:
        copy.wait()
    pay_ref[0:H, :] = jnp.transpose(w_mid[0, 0].astype(F32)).astype(BF16)


def small_rows(ref):
    return [ref[2 - p, H:ROWS, :].astype(F32) for p in range(3)]


def tables(smalls):
    return [(s[0:8] + s[8:16]) + s[16:24] for s in smalls]


def gather_rows(chunk_ref, layout, points):
    blank = jnp.zeros((8, SPAN), F32)
    for c, regions in enumerate(layout):
        parts = []
        for big_a, big_b in regions:
            p = 0 if big_a == 0 else 2 if big_a == 4 else 1
            q = 0 if big_b == 0 else 2 if big_b == 4 else 1
            at = PLACE[(2, big_a - 1, 0)[p], (0, big_b - 1, 2)[q]]
            parts.append(points[q][p][:, at : at + SPAN])
        parts += [blank] * (4 - len(parts))
        chunk_ref[c] = jnp.concatenate(parts, axis=1)
    for c in range(len(layout), 8):
        chunk_ref[c] = jnp.zeros((8, LANES), F32)
    return [chunk_ref[:, k, :] for k in range(8)]


def frame(layout, flag):
    spot = lax.broadcasted_iota(jnp.int32, (8, LANES), 0) * 4 + (
        lax.broadcasted_iota(jnp.int32, (8, LANES), 1) // SPAN
    )

    def among(test):
        hit = jnp.zeros((8, LANES), F32)
        for c, regions in enumerate(layout):
            for k, region in enumerate(regions):
                if test(region):
                    hit = jnp.where(spot == 4 * c + k, 1.0, hit)
        return hit

    off_x = among(lambda r: r[0] == 4) - among(lambda r: r[0] == 0)
    off_y = among(lambda r: r[1] == 4) - among(lambda r: r[1] == 0)
    own = (1.0 - off_x * off_x) * (1.0 - off_y * off_y)
    wide_x = DELTA + (1.0 - 3.0 * DELTA) * among(lambda r: r[0] == 2)
    wide_y = DELTA + (1.0 - 3.0 * DELTA) * among(lambda r: r[1] == 2)
    return off_x, off_y, wide_x * wide_y / SPAN * flag, own


def put_coefs(coef_ref, rows, off_x, off_y, nets, small):
    pos_x, pos_y, diff, vel_x, vel_y, rate = rows[:6]
    way = small[30:31, 0:LANES]
    coords_x = {p: pos_x + (off_x - float(p)) for p, _, _ in nets}
    coords_y = {q: pos_y + way * (off_y - float(q)) for _, q, _ in nets}
    bumps_x = {p: bump(t) for p, t in coords_x.items()}
    bumps_y = {q: bump(s) for q, s in coords_y.items()}
    for n, (p, q, present) in enumerate(nets):
        b_x, b_y = bumps_x[p], bumps_y[q]
        window = b_x[0] * b_y[0] * present
        window_x = b_x[1] * b_y[0] * present
        window_y = b_x[0] * b_y[1] * present
        window_l = (b_x[2] * b_y[0] + b_x[0] * b_y[2]) * present
        coef_ref[n, 0] = 2.0 * coords_x[p] - 1.0
        coef_ref[n, 1] = 2.0 * coords_y[q] - 1.0
        coef_ref[n, 2] = (
            -diff * window_l + vel_x * window_x + vel_y * window_y - rate * window
        )
        coef_ref[n, 3] = -2.0 * diff * window_x + vel_x * window
        coef_ref[n, 4] = -2.0 * diff * window_y + vel_y * window
        coef_ref[n, 5] = -diff * window
    left = lax.broadcasted_iota(jnp.int32, (8, LANES), 1) < LANES // 2
    for k in range(6):
        coef_ref[len(nets), k] = jnp.where(left, coef_ref[0, k], coef_ref[2, k])


def spread(smalls, par_ref):
    lane = lax.broadcasted_iota(jnp.int32, (8, 5 * LANES), 1) // LANES
    line = lax.broadcasted_iota(jnp.int32, (8, 5 * LANES), 0)
    pick = jnp.where(lane == line, 1.0, 0.0).astype(BF16)
    for n, small in enumerate(smalls):
        wide = lax.dot_general(
            small[24:32].astype(BF16),
            pick,
            (((0,), (0,)), ((), ())),
            preferred_element_type=F32,
        )
        for k in range(5):
            par_ref[n, k] = wide[:, LANES * k : LANES * k + LANES]
        w_first, w_second = wide[:, 0:LANES], wide[:, LANES : 2 * LANES]
        par_ref[n, 5] = -8.0 * (w_first * w_first + w_second * w_second)


def forward(par_ref, n, weights, xi, eta):
    w_first, w_second = par_ref[n, 0], par_ref[n, 1]
    h1 = jnp.tanh(xi * w_first + eta * w_second + par_ref[n, 2])
    d1 = 1.0 - h1 * h1
    d1x2 = 2.0 * d1
    streams = jnp.concatenate(
        [
            h1.astype(BF16),
            (d1x2 * w_first).astype(BF16),
            (d1x2 * w_second).astype(BF16),
            (h1 * d1 * par_ref[n, 5]).astype(BF16),
        ],
        axis=1,
    )
    mixed = [jnp.dot(w, streams, preferred_element_type=F32) for w in weights]
    if len(mixed) == 2:
        lane = lax.broadcasted_iota(jnp.int32, (1, 4 * LANES), 1)
        mixed = [jnp.where(lane % LANES < LANES // 2, *mixed)]
    mixed = mixed[0]
    h2 = jnp.tanh(mixed[:, 0:LANES] + par_ref[n, 3])
    gx = mixed[:, LANES : 2 * LANES]
    gy = mixed[:, 2 * LANES : 3 * LANES]
    curve = mixed[:, 3 * LANES :]
    return h1, streams, h2, gx, gy, curve


def coefs(coef_ref, n, c):
    return [coef_ref[n, k, c : c + 1, :] for k in range(6)]


def add_field(total_ref, c, mix, head):
    total_ref[c : c + 1, :] += jnp.sum(mix * head, axis=0, keepdims=True)


def near_step(total_ref, coef_ref, n, c, par_ref, m, weights):
    xi, eta, c0, c1, c2, c3 = coefs(coef_ref, n, c)
    _, _, h2, gx, gy, curve = forward(par_ref, m, weights, xi, eta)
    d2 = 1.0 - h2 * h2
    square = gx * gx + gy * gy
    inner = c1 * gx + c2 * gy + c3 * (curve - 2.0 * h2 * square)
    add_field(total_ref, c, c0 * h2 + d2 * inner, par_ref[m, 4])


def own_step(total_ref, coef_ref, n, c, par_ref, weights, k, s_ref, state_ref):
    xi, eta, c0, c1, c2, c3 = coefs(coef_ref, n, c)
    h1, streams, h2, gx, gy, curve = forward(par_ref, 1, weights, xi, eta)
    d2 = 1.0 - h2 * h2
    square = gx * gx + gy * gy
    inner = c1 * gx + c2 * gy + c3 * (curve - 2.0 * h2 * square)
    mix = c0 * h2 + d2 * inner
    head = par_ref[1, 4]
    add_field(total_ref, c, mix, head)
    turn = (4.0 * c3) * h2
    s_ref[k] = streams
    state_ref[k, 0] = h1
    state_ref[k, 1] = mix
    state_ref[k, 2] = head * d2
    state_ref[k, 3] = c0 - 2.0 * (d2 * square * c3 + h2 * inner)
    state_ref[k, 4] = c1 - turn * gx
    state_ref[k, 5] = c2 - turn * gy


def middle_kernel(
    mid_ref, tab_ref, par_ref, coef_ref, info_ref, s_ref, state_ref, chunk_ref, total_ref
):
    smalls = small_rows(mid_ref)
    points = tables(smalls)
    points[1] = tab_ref[...]
    rows = gather_rows(chunk_ref, MIDDLE, [None, points, None])
    off_x, off_y, area, own = frame(MIDDLE, rows[7])
    nets = [(p - 1, 0, smalls[p][29:30, 0:LANES]) for p in range(3)]
    put_coefs(coef_ref, rows, off_x, off_y, nets, smalls[1])
    spread(smalls, par_ref)
    left = lax.broadcasted_iota(jnp.int32, (H, LANES), 1) < LANES // 2
    for k in range(6):
        par_ref[3, k] = jnp.where(left, par_ref[0, k], par_ref[2, k])
    total_ref[...] = jnp.zeros((8, LANES), F32)
    weights = [mid_ref[2 - p, 0:H, :] for p in range(3)]
    for c in range(3):
        own_step(total_ref, coef_ref, 1, c, par_ref, weights[1:2], c, s_ref, state_ref)
    for c in range(3):
        near_step(total_ref, coef_ref, 3, c, par_ref, 3, weights[0::2])
    info_ref[0] = total_ref[...]
    info_ref[1] = area
    info_ref[2] = rows[6]
    info_ref[3] = own


def side(layout, q, mid_ref, side_ref, own_table, par_ref, work):
    coef_ref, total_ref, side_par, chunk_ref, s_ref, state_ref = work
    smalls = small_rows(mid_ref)
    far = small_rows(side_ref)
    points = [None, tables(smalls), None]
    if own_table is not None:
        points[1][1] = own_table
    points[1 + q] = tables(far)
    rows = gather_rows(chunk_ref, layout, points)
    off_x, off_y, area, own = frame(layout, rows[7])
    nets = [(p - 1, 0, smalls[p][29:30, 0:LANES]) for p in range(3)]
    nets += [(p - 1, q, far[p][29:30, 0:LANES]) for p in range(3)]
    put_coefs(coef_ref, rows, off_x, off_y, nets, smalls[1])
    spread(far, side_par)
    total_ref[...] = jnp.zeros((8, LANES), F32)
    weights = [mid_ref[2 - p, 0:H, :] for p in range(3)]
    for k in range(2):
        own_step(
            total_ref, coef_ref, 1, 3 + k, par_ref, weights[1:2], k, s_ref, state_ref
        )
    near_step(total_ref, coef_ref, 6, 3, par_ref, 3, weights[0::2])
    for p, c in ((0, 0), (1, 0), (1, 1), (2, 1), (1, 2)):
        near_step(total_ref, coef_ref, 3 + p, c, side_par, p, [side_ref[2 - p, 0:H, :]])
    return area, rows[6], own


def moved(total, layout, target):
    places = {}
    for c, regions in enumerate(layout[:3]):
        for k, region in enumerate(regions):
            places[region] = (c, SPAN * k)
    rows = []
    for regions in target:
        parts = []
        for region in regions:
            if region in places:
                c, at = places[region]
                parts.append(total[c : c + 1, at : at + SPAN])
            else:
                parts.append(jnp.zeros((1, SPAN), F32))
        parts += [jnp.zeros((1, SPAN), F32)] * (4 - len(parts))
        rows.append(jnp.concatenate(parts, axis=1))
    return jnp.concatenate(rows + [jnp.zeros((8 - len(rows), LANES), F32)], axis=0)


def joined(one, first, last, two):
    blank = jnp.zeros((6 - (last - first), LANES), F32)
    return jnp.concatenate([one[first:last], two[3:5], blank], axis=0)


def residuals(info_m, first, last, here, total_ref, layout, target):
    area_s, source_s, own_s = here
    totals = total_ref[...]
    area = joined(info_m[1], first, last, area_s)
    source = joined(info_m[2], first, last, source_s)
    own = joined(info_m[3], first, last, own_s)
    total = joined(info_m[0], first, last, totals) + moved(totals, layout, target)
    residual = total - source
    total_ref[...] = 2.0 * area * residual
    return own * area * residual * residual


def put(ref, parts, base):
    value = functools.reduce(lambda one, two: one + two, parts)
    value = value if base is None else base[...] + value
    ref[...] = value
    return value


def backward(places, groups, total_ref, par_ref, w_ref, d_ref, acc_ref, gw_ref, base):
    w1, w2, pw = par_ref.at[1, 0], par_ref.at[1, 1], par_ref.at[1, 5]

    def start(k, g):
        return acc_ref.at[k] if g else None if base is None else base[0].at[k]

    def cotangents(g):
        d_bases, mixes = [], []
        for row in groups[g]:
            coef_ref, c, _, state_ref, k = places[row]
            c3 = coef_ref[1, 5, c : c + 1, :]
            adjoint = total_ref[row : row + 1, :]
            scale = state_ref[k, 2] * adjoint
            d_base = scale * state_ref[k, 3]
            d_bases.append(d_base)
            mixes.append(state_ref[k, 1] * adjoint)
            d_ref[row, :, 0:LANES] = d_base.astype(BF16)
            d_ref[row, :, LANES : 2 * LANES] = (scale * state_ref[k, 4]).astype(BF16)
            d_ref[row, :, 2 * LANES : 3 * LANES] = (scale * state_ref[k, 5]).astype(BF16)
            d_ref[row, :, 3 * LANES :] = (scale * c3).astype(BF16)
        put(acc_ref.at[4], d_bases, start(4, g))
        put(acc_ref.at[5], mixes, start(5, g))

    cotangents(0)
    for g, group in enumerate(groups):
        d_streams = [
            jnp.dot(w_ref[0, 0], d_ref[row], preferred_element_type=F32) for row in group
        ]
        terms = [
            lax.dot_general(
                places[row][2][places[row][4]],
                d_ref[row],
                (((1,), (1,)), ((), ())),
                preferred_element_type=F32,
            )
            for row in group
        ]
        if g + 1 < len(groups):
            cotangents(g + 1)
        grad_w = put(gw_ref, terms, gw_ref if g else None if base is None else base[1])
        norm = jnp.sum(grad_w * grad_w)
        parts = [[], [], [], []]
        for row, ds in zip(group, d_streams):
            coef_ref, c, _, state_ref, k = places[row]
            xi, eta = coef_ref[1, 0, c : c + 1, :], coef_ref[1, 1, c : c + 1, :]
            h1 = state_ref[k, 0]
            ds0, ds1 = ds[:, 0:LANES], ds[:, LANES : 2 * LANES]
            ds2, ds3 = ds[:, 2 * LANES : 3 * LANES], ds[:, 3 * LANES :]
            d1 = 1.0 - h1 * h1
            cross = w1[...] * ds1 + w2[...] * ds2
            d_pre = d1 * (ds0 + pw[...] * ds3 * (3.0 * d1 - 2.0) - (4.0 * h1) * cross)
            d1x2 = 2.0 * d1
            parts[0].append(d1x2 * ds1 + xi * d_pre)
            parts[1].append(d1x2 * ds2 + eta * d_pre)
            parts[2].append(d_pre)
            parts[3].append(h1 * d1 * ds3)
        for k, part in enumerate(parts):
            put(acc_ref.at[k], part, start(k, g))
    return norm


def high_kernel(
    mid_ref,
    hi_ref,
    tab_ref,
    w_ref,
    par_ref,
    coef_m,
    info_m,
    s_m,
    state_m,
    acc_ref,
    gw_ref,
    loss_ref,
    coef_ref,
    s_ref,
    state_ref,
    side_par,
    chunk_ref,
    total_ref,
    d_ref,
):
    work = (coef_ref, total_ref, side_par, chunk_ref, s_ref, state_ref)
    here = side(HIGH, 1, mid_ref, hi_ref, tab_ref[...], par_ref, work)
    loss_ref[...] = residuals(info_m, 0, 2, here, total_ref, HIGH, EARLY)
    places = [(coef_m, c, s_m, state_m, c) for c in range(2)]
    places += [(coef_ref, 3 + k, s_ref, state_ref, k) for k in range(2)]
    backward(
        places, ((0, 1), (2, 3)), total_ref, par_ref, w_ref, d_ref, acc_ref, gw_ref, None
    )


def last_kernel(
    mid_ref,
    lo_ref,
    w_ref,
    par_ref,
    coef_m,
    info_m,
    s_m,
    state_m,
    acc_h,
    gw_h,
    loss_h,
    gw_ref,
    gs_ref,
    stat_ref,
    coef_ref,
    s_ref,
    state_ref,
    side_par,
    chunk_ref,
    total_ref,
    d_ref,
    acc_ref,
):
    work = (coef_ref, total_ref, side_par, chunk_ref, s_ref, state_ref)
    here = side(BELOW, -1, mid_ref, lo_ref, None, par_ref, work)
    loss = jnp.sum(
        loss_h[...] + residuals(info_m, 2, 3, here, total_ref, BELOW, LATE)
    )
    places = [(coef_m, 2, s_m, state_m, 2)]
    places += [(coef_ref, 3 + k, s_ref, state_ref, k) for k in range(2)]
    base = (acc_h, gw_h)
    norm = backward(
        places, ((0, 1, 2),), total_ref, par_ref, w_ref, d_ref, acc_ref, gw_ref, base
    )
    sums = [jnp.sum(acc_ref[k], axis=1, keepdims=True) for k in range(6)]
    turn = -16.0 * sums[3]
    grid = jnp.concatenate(
        [
            sums[0] + turn * par_ref[1, 0, :, 0:1],
            sums[1] + turn * par_ref[1, 1, :, 0:1],
            sums[2],
            sums[4],
            sums[5],
            jnp.zeros((H, 3), F32),
        ],
        axis=1,
    )
    gs_ref[...] = jnp.transpose(grid)
    square = norm + jnp.sum(grid * grid)
    lane = lax.broadcasted_iota(jnp.int32, stat_ref.shape, 2)
    stat_ref[...] = jnp.where(lane == 0, square, jnp.where(lane == 1, loss, 0.0))


def sum_kernel(got_ref, out_ref):
    total = jnp.sum(got_ref[...], axis=0, keepdims=True)
    out_ref[...] = jnp.broadcast_to(total, out_ref.shape)


def scale_kernel(nets, got_ref, gw_ref, gs_ref, o0, o1, o2, o3, o4, loss_ref):
    total = jnp.sum(got_ref[...], axis=0)
    rms = jnp.sqrt(total[:, 0:1] / (nets * (H * H + 5 * H)) + EPS)
    inverse = 1.0 / rms
    gs = gs_ref[...] * inverse
    o0[0, 0] = gs[0:2]
    o1[0] = gs[2:3]
    o2[0, 0] = gw_ref[...] * inverse
    o3[0] = gs[3:4]
    o4[0] = gs[4:5]
    loss_ref[...] = total[:, 1:2]


def call(kernel, outs, scratch=(), limit=16 << 20, flops=0, place=pltpu.VMEM):
    extra = {}
    if place != pltpu.VMEM:
        extra["in_specs"] = [pl.BlockSpec(memory_space=place)] * 10
    return pl.pallas_call(
        kernel,
        out_shape=outs,
        scratch_shapes=scratch,
        compiler_params=pltpu.CompilerParams(vmem_limit_bytes=limit),
        cost_estimate=pl.CostEstimate(
            flops=flops, bytes_accessed=1 << 18, transcendentals=0
        ),
        **extra,
    )


def shape(dims, kind=F32):
    return jax.ShapeDtypeStruct(dims, kind)


GX = ("z", "yh", "c")
GY = ("yl", "x")
FIRST = ("z", "c")
SECOND = ("yh", "yl", "x")


def local(
    points,
    diffusion,
    drift,
    ionization,
    source,
    in_weight,
    in_bias,
    mid_weight,
    mid_bias,
    out_weight,
):
    count_x = lax.axis_size(GX)
    count_y = lax.axis_size(GY)
    inputs = (
        points.transpose(1, 2, 0, 3),
        diffusion,
        drift.transpose(1, 2, 0, 3),
        ionization,
        source,
        in_weight,
        in_bias,
        mid_weight,
        mid_bias,
        out_weight,
    )
    payload, table = call(
        pack_kernel,
        (shape((ROWS, H), BF16), shape((8, 384))),
        tuple(pltpu.VMEM(x.shape, x.dtype) for x in inputs)
        + (pltpu.SemaphoreType.DMA((13,)),),
        place=pl.ANY,
        limit=16 << 20,
    )(*(pltpu.with_memory_space_constraint(x, pltpu.HBM) for x in inputs))
    forth = [(i, i + 1) for i in range(count_x - 1)]
    after = lax.ppermute(payload, GX, [(j, i) for i, j in forth])
    before = lax.ppermute(payload, GX, forth)
    row = jnp.stack([after, payload, before])
    pairs = [(i, i ^ 1) for i in range(count_y)]
    bonds = [(i, (i + 1) % count_y) for i in range(1, count_y, 2)]
    above = lax.ppermute(row, GY, pairs)
    below = lax.ppermute(row, GY, bonds + [(j, i) for i, j in bonds])
    first = lax.axis_size(FIRST)
    second = lax.axis_size(SECOND)

    def kept(chunks):
        return ((chunks, H, 4 * LANES), BF16), ((chunks, 6, H, LANES), F32)

    chunk = pltpu.VMEM((8, 8, LANES), F32)
    total = pltpu.VMEM((8, LANES), F32)
    accs = (6, H, LANES)
    params, *middle = call(
        middle_kernel,
        (shape((4, 6, H, LANES)), shape((4, 6, 8, LANES)), shape((4, 8, LANES)))
        + tuple(shape(*k) for k in kept(3)),
        (chunk, total),
        flops=10**9,
    )(row, table)

    def scratch(chunks):
        return (
            pltpu.VMEM((7, 6, 8, LANES), F32),
            *(pltpu.VMEM(*k) for k in kept(2)),
            pltpu.VMEM((3, 6, H, LANES), F32),
            chunk,
            total,
            pltpu.VMEM((chunks, H, 4 * LANES), BF16),
        )

    high = call(
        high_kernel,
        (shape(accs), shape((H, H)), shape((8, LANES))),
        scratch(4),
        limit=20 << 20,
        flops=10**9,
    )(row, above, table, mid_weight, params, *middle)
    grad_w, grad_s, stat = call(
        last_kernel,
        (shape((H, H)), shape((8, H)), shape((first, 1, LANES))),
        scratch(3) + (pltpu.VMEM(accs, F32),),
        limit=20 << 20,
        flops=10**9,
    )(row, below, mid_weight, params, *middle, *high)
    got = lax.all_to_all(stat, FIRST, 0, 0, tiled=True)
    part = call(sum_kernel, shape((second, 1, LANES)))(got)
    got = lax.all_to_all(part, SECOND, 0, 0, tiled=True)
    outs = call(
        lambda *refs: scale_kernel(count_x * count_y, *refs),
        (
            shape((1, 1, 2, H)),
            shape((1, 1, H)),
            shape((1, 1, H, H)),
            shape((1, 1, H)),
            shape((1, 1, H)),
            shape((1, 1)),
        ),
    )(got, grad_w, grad_s)
    return (*outs[:5], outs[5].reshape(()))


def solution(mesh):
    fine = Mesh(
        mesh.devices.reshape(8, 2, 2, 4, 4), ("z", "yh", "c", "yl", "x")
    )
    return jax.shard_map(
        local,
        mesh=fine,
        in_specs=(
            P(None, GX, GY, None),
            P(GX, GY, None),
            P(None, GX, GY, None),
            P(GX, GY, None),
            P(GX, GY, None),
            P(GX, GY, None, None),
            P(GX, GY, None),
            P(GX, GY, None, None),
            P(GX, GY, None),
            P(GX, GY, None),
        ),
        out_specs=(
            P(GX, GY, None, None),
            P(GX, GY, None),
            P(GX, GY, None, None),
            P(GX, GY, None),
            P(GX, GY, None),
            P(),
        ),
        check_vma=False,
    )
```

```python
import functools

import jax
import jax.numpy as jnp
from jax import lax
from jax.experimental import pallas as pl
from jax.experimental.pallas import tpu as pltpu
from jax.sharding import Mesh, PartitionSpec as P

DELTA = 0.25
EPS = 1e-06
H = 256
LANES = 128
SPAN = 32
ROWS = 288
F32 = jnp.float32
BF16 = jnp.bfloat16

MIDDLE = (
    ((0, 2), (1, 2), (3, 2), (4, 2)),
    ((0, 3), (1, 3), (3, 3), (4, 3)),
    ((0, 1), (1, 1), (3, 1), (4, 1)),
)
HIGH = (
    ((0, 3), (0, 4), (1, 3), (1, 4)),
    ((3, 3), (3, 4), (4, 3), (4, 4)),
    ((2, 3), (2, 4)),
    ((0, 4), (1, 4), (3, 4), (4, 4)),
    ((2, 2), (2, 3), (2, 4)),
)
BELOW = (
    ((0, 0), (0, 1), (1, 0), (1, 1)),
    ((3, 0), (3, 1), (4, 0), (4, 1)),
    ((2, 0), (2, 1)),
    ((0, 0), (1, 0), (3, 0), (4, 0)),
    ((2, 0), (2, 1)),
)
EARLY = (MIDDLE[0], MIDDLE[1], HIGH[3], HIGH[4])
LATE = (MIDDLE[2], BELOW[3], BELOW[4])
PLACE = {
    (0, 0): 0,
    (0, 1): 32,
    (0, 2): 64,
    (1, 0): 96,
    (2, 0): 128,
    (2, 1): 160,
    (2, 2): 192,
    (1, 2): 224,
    (1, 1): 256,
}
LOW = (0.0, DELTA, 1.0 - DELTA)
WIDTH = (DELTA, 1.0 - 2.0 * DELTA, DELTA)


def smooth_rise(coord):
    ramp = jnp.clip((coord + DELTA) / (2.0 * DELTA), 0.0, 1.0)
    value = ramp * ramp * ramp * (10.0 - 15.0 * ramp + 6.0 * ramp * ramp)
    slope = 30.0 * ramp * ramp * (1.0 - ramp) * (1.0 - ramp) / (2.0 * DELTA)
    bend = 60.0 * ramp * (1.0 - ramp) * (1.0 - 2.0 * ramp) / (4.0 * DELTA * DELTA)
    return (value, slope, bend)


def bump(coord):
    rise_a = smooth_rise(coord)
    rise_b = smooth_rise(coord - 1.0)
    return (rise_a[0] - rise_b[0], rise_a[1] - rise_b[1], rise_a[2] - rise_b[2])


def pack_kernel(*refs):
    sources, (pay_ref, tab_ref), buffers, sems = (
        refs[:10],
        refs[10:12],
        refs[12:22],
        refs[22],
    )
    pts, dif, dri, ion, src, w_in, b_in, w_mid, b_mid, w_out = buffers
    strips = [pl.ds(64 * k, 64) for k in range(4)]
    pairs = [(sources[7].at[0, 0, k], w_mid.at[0, 0, k]) for k in strips]
    pairs += [(sources[k], buffers[k]) for k in range(10) if k != 7]
    copies = [
        pltpu.make_async_copy(one, two, sems.at[k]) for k, (one, two) in enumerate(pairs)
    ]
    for copy in copies:
        copy.start()
    for copy in copies[4:]:
        copy.wait()
    zeros = jnp.zeros((1, SPAN), F32)
    ones = jnp.ones((1, SPAN), F32)
    pieces = {}
    for a in range(3):
        for b in range(3):
            rows = [
                LOW[a] + WIDTH[a] * pts[a, b, 0:1, :],
                LOW[b] + WIDTH[b] * pts[a, b, 1:2, :],
                dif[a, b : b + 1, :],
                dri[a, b, 0:1, :],
                dri[a, b, 1:2, :],
                ion[a, b : b + 1, :],
                src[a, b : b + 1, :],
                ones,
            ]
            pieces[a, b] = jnp.concatenate(rows, axis=0)
    blank = jnp.concatenate([zeros] * 8, axis=0)
    turn = lax.rem(lax.axis_index("x"), 2) == 1
    placed = {
        at: jnp.where(turn, pieces[a, 2 - b], pieces[a, b]) for (a, b), at in PLACE.items()
    }
    order = [placed.get(32 * k, blank) for k in range(12)]
    tabs = [jnp.concatenate(order[4 * k : 4 * k + 4], axis=1) for k in range(3)]
    for k in range(3):
        tab_ref[:, 128 * k : 128 * k + 128] = tabs[k]
    edge = jnp.concatenate(tabs[:2], axis=1)
    high = edge.astype(BF16).astype(F32)
    rest = edge - high
    mid = rest.astype(BF16).astype(F32)
    low = rest - mid
    small = jnp.concatenate(
        [
            w_in[0, 0].astype(F32),
            b_in[0].astype(F32),
            b_mid[0].astype(F32),
            w_out[0].astype(F32),
            jnp.ones((1, H), F32),
            jnp.where(turn, -1.0, 1.0) * jnp.ones((1, H), F32),
            jnp.zeros((1, H), F32),
        ],
        axis=0,
    )
    pay_ref[H:ROWS, :] = jnp.concatenate([high, mid, low, small], axis=0).astype(BF16)
    for copy in copies[:4]:
        copy.wait()
    pay_ref[0:H, :] = jnp.transpose(w_mid[0, 0].astype(F32)).astype(BF16)


def small_rows(ref):
    return [ref[2 - p, H:ROWS, :].astype(F32) for p in range(3)]


def tables(smalls):
    return [(s[0:8] + s[8:16]) + s[16:24] for s in smalls]


def gather_rows(chunk_ref, layout, points):
    blank = jnp.zeros((8, SPAN), F32)
    for c, regions in enumerate(layout):
        parts = []
        for big_a, big_b in regions:
            p = 0 if big_a == 0 else 2 if big_a == 4 else 1
            q = 0 if big_b == 0 else 2 if big_b == 4 else 1
            at = PLACE[(2, big_a - 1, 0)[p], (0, big_b - 1, 2)[q]]
            parts.append(points[q][p][:, at : at + SPAN])
        parts += [blank] * (4 - len(parts))
        chunk_ref[c] = jnp.concatenate(parts, axis=1)
    for c in range(len(layout), 8):
        chunk_ref[c] = jnp.zeros((8, LANES), F32)
    return [chunk_ref[:, k, :] for k in range(8)]


def frame(layout, flag):
    spot = lax.broadcasted_iota(jnp.int32, (8, LANES), 0) * 4 + (
        lax.broadcasted_iota(jnp.int32, (8, LANES), 1) // SPAN
    )

    def among(test):
        hit = jnp.zeros((8, LANES), F32)
        for c, regions in enumerate(layout):
            for k, region in enumerate(regions):
                if test(region):
                    hit = jnp.where(spot == 4 * c + k, 1.0, hit)
        return hit

    off_x = among(lambda r: r[0] == 4) - among(lambda r: r[0] == 0)
    off_y = among(lambda r: r[1] == 4) - among(lambda r: r[1] == 0)
    own = (1.0 - off_x * off_x) * (1.0 - off_y * off_y)
    wide_x = DELTA + (1.0 - 3.0 * DELTA) * among(lambda r: r[0] == 2)
    wide_y = DELTA + (1.0 - 3.0 * DELTA) * among(lambda r: r[1] == 2)
    return off_x, off_y, wide_x * wide_y / SPAN * flag, own


def put_coefs(coef_ref, rows, off_x, off_y, nets, small):
    pos_x, pos_y, diff, vel_x, vel_y, rate = rows[:6]
    way = small[30:31, 0:LANES]
    coords_x = {p: pos_x + (off_x - float(p)) for p, _, _ in nets}
    coords_y = {q: pos_y + way * (off_y - float(q)) for _, q, _ in nets}
    bumps_x = {p: bump(t) for p, t in coords_x.items()}
    bumps_y = {q: bump(s) for q, s in coords_y.items()}
    for n, (p, q, present) in enumerate(nets):
        b_x, b_y = bumps_x[p], bumps_y[q]
        window = b_x[0] * b_y[0] * present
        window_x = b_x[1] * b_y[0] * present
        window_y = b_x[0] * b_y[1] * present
        window_l = (b_x[2] * b_y[0] + b_x[0] * b_y[2]) * present
        coef_ref[n, 0] = 2.0 * coords_x[p] - 1.0
        coef_ref[n, 1] = 2.0 * coords_y[q] - 1.0
        coef_ref[n, 2] = (
            -diff * window_l + vel_x * window_x + vel_y * window_y - rate * window
        )
        coef_ref[n, 3] = -2.0 * diff * window_x + vel_x * window
        coef_ref[n, 4] = -2.0 * diff * window_y + vel_y * window
        coef_ref[n, 5] = -diff * window
    left = lax.broadcasted_iota(jnp.int32, (8, LANES), 1) < LANES // 2
    for k in range(6):
        coef_ref[len(nets), k] = jnp.where(left, coef_ref[0, k], coef_ref[2, k])


def spread(smalls, par_ref):
    lane = lax.broadcasted_iota(jnp.int32, (8, 5 * LANES), 1) // LANES
    line = lax.broadcasted_iota(jnp.int32, (8, 5 * LANES), 0)
    pick = jnp.where(lane == line, 1.0, 0.0).astype(BF16)
    for n, small in enumerate(smalls):
        wide = lax.dot_general(
            small[24:32].astype(BF16),
            pick,
            (((0,), (0,)), ((), ())),
            preferred_element_type=F32,
        )
        for k in range(5):
            par_ref[n, k] = wide[:, LANES * k : LANES * k + LANES]
        w_first, w_second = wide[:, 0:LANES], wide[:, LANES : 2 * LANES]
        par_ref[n, 5] = -8.0 * (w_first * w_first + w_second * w_second)


def forward(par_ref, n, weights, xi, eta):
    w_first, w_second = par_ref[n, 0], par_ref[n, 1]
    h1 = jnp.tanh(xi * w_first + eta * w_second + par_ref[n, 2])
    d1 = 1.0 - h1 * h1
    d1x2 = 2.0 * d1
    streams = jnp.concatenate(
        [
            h1.astype(BF16),
            (d1x2 * w_first).astype(BF16),
            (d1x2 * w_second).astype(BF16),
            (h1 * d1 * par_ref[n, 5]).astype(BF16),
        ],
        axis=1,
    )
    mixed = [jnp.dot(w, streams, preferred_element_type=F32) for w in weights]
    if len(mixed) == 2:
        lane = lax.broadcasted_iota(jnp.int32, (1, 4 * LANES), 1)
        mixed = [jnp.where(lane % LANES < LANES // 2, *mixed)]
    mixed = mixed[0]
    h2 = jnp.tanh(mixed[:, 0:LANES] + par_ref[n, 3])
    gx = mixed[:, LANES : 2 * LANES]
    gy = mixed[:, 2 * LANES : 3 * LANES]
    curve = mixed[:, 3 * LANES :]
    return h1, streams, h2, gx, gy, curve


def coefs(coef_ref, n, c):
    return [coef_ref[n, k, c : c + 1, :] for k in range(6)]


def add_field(total_ref, c, mix, head):
    total_ref[c : c + 1, :] += jnp.sum(mix * head, axis=0, keepdims=True)


def near_step(total_ref, coef_ref, n, c, par_ref, m, weights):
    xi, eta, c0, c1, c2, c3 = coefs(coef_ref, n, c)
    _, _, h2, gx, gy, curve = forward(par_ref, m, weights, xi, eta)
    d2 = 1.0 - h2 * h2
    square = gx * gx + gy * gy
    inner = c1 * gx + c2 * gy + c3 * (curve - 2.0 * h2 * square)
    add_field(total_ref, c, c0 * h2 + d2 * inner, par_ref[m, 4])


def own_step(total_ref, coef_ref, n, c, par_ref, weights, k, s_ref, state_ref):
    xi, eta, c0, c1, c2, c3 = coefs(coef_ref, n, c)
    h1, streams, h2, gx, gy, curve = forward(par_ref, 1, weights, xi, eta)
    d2 = 1.0 - h2 * h2
    square = gx * gx + gy * gy
    inner = c1 * gx + c2 * gy + c3 * (curve - 2.0 * h2 * square)
    mix = c0 * h2 + d2 * inner
    head = par_ref[1, 4]
    add_field(total_ref, c, mix, head)
    turn = (4.0 * c3) * h2
    s_ref[k] = streams
    state_ref[k, 0] = h1
    state_ref[k, 1] = mix
    state_ref[k, 2] = head * d2
    state_ref[k, 3] = c0 - 2.0 * (d2 * square * c3 + h2 * inner)
    state_ref[k, 4] = c1 - turn * gx
    state_ref[k, 5] = c2 - turn * gy


def middle_kernel(
    mid_ref, tab_ref, par_ref, coef_ref, info_ref, s_ref, state_ref, chunk_ref, total_ref
):
    smalls = small_rows(mid_ref)
    points = tables(smalls)
    points[1] = tab_ref[...]
    rows = gather_rows(chunk_ref, MIDDLE, [None, points, None])
    off_x, off_y, area, own = frame(MIDDLE, rows[7])
    nets = [(p - 1, 0, smalls[p][29:30, 0:LANES]) for p in range(3)]
    put_coefs(coef_ref, rows, off_x, off_y, nets, smalls[1])
    spread(smalls, par_ref)
    left = lax.broadcasted_iota(jnp.int32, (H, LANES), 1) < LANES // 2
    for k in range(6):
        par_ref[3, k] = jnp.where(left, par_ref[0, k], par_ref[2, k])
    total_ref[...] = jnp.zeros((8, LANES), F32)
    weights = [mid_ref[2 - p, 0:H, :] for p in range(3)]
    for c in range(3):
        own_step(total_ref, coef_ref, 1, c, par_ref, weights[1:2], c, s_ref, state_ref)
    for c in range(3):
        near_step(total_ref, coef_ref, 3, c, par_ref, 3, weights[0::2])
    info_ref[0] = total_ref[...]
    info_ref[1] = area
    info_ref[2] = rows[6]
    info_ref[3] = own


def side(layout, q, mid_ref, side_ref, own_table, par_ref, work):
    coef_ref, total_ref, side_par, chunk_ref, s_ref, state_ref = work
    smalls = small_rows(mid_ref)
    far = small_rows(side_ref)
    points = [None, tables(smalls), None]
    if own_table is not None:
        points[1][1] = own_table
    points[1 + q] = tables(far)
    rows = gather_rows(chunk_ref, layout, points)
    off_x, off_y, area, own = frame(layout, rows[7])
    nets = [(p - 1, 0, smalls[p][29:30, 0:LANES]) for p in range(3)]
    nets += [(p - 1, q, far[p][29:30, 0:LANES]) for p in range(3)]
    put_coefs(coef_ref, rows, off_x, off_y, nets, smalls[1])
    spread(far, side_par)
    total_ref[...] = jnp.zeros((8, LANES), F32)
    weights = [mid_ref[2 - p, 0:H, :] for p in range(3)]
    for k in range(2):
        own_step(
            total_ref, coef_ref, 1, 3 + k, par_ref, weights[1:2], k, s_ref, state_ref
        )
    near_step(total_ref, coef_ref, 6, 3, par_ref, 3, weights[0::2])
    for p, c in ((0, 0), (1, 0), (1, 1), (2, 1), (1, 2)):
        near_step(total_ref, coef_ref, 3 + p, c, side_par, p, [side_ref[2 - p, 0:H, :]])
    return area, rows[6], own


def moved(total, layout, target):
    places = {}
    for c, regions in enumerate(layout[:3]):
        for k, region in enumerate(regions):
            places[region] = (c, SPAN * k)
    rows = []
    for regions in target:
        parts = []
        for region in regions:
            if region in places:
                c, at = places[region]
                parts.append(total[c : c + 1, at : at + SPAN])
            else:
                parts.append(jnp.zeros((1, SPAN), F32))
        parts += [jnp.zeros((1, SPAN), F32)] * (4 - len(parts))
        rows.append(jnp.concatenate(parts, axis=1))
    return jnp.concatenate(rows + [jnp.zeros((8 - len(rows), LANES), F32)], axis=0)


def joined(one, first, last, two):
    blank = jnp.zeros((6 - (last - first), LANES), F32)
    return jnp.concatenate([one[first:last], two[3:5], blank], axis=0)


def residuals(info_m, first, last, here, total_ref, layout, target):
    area_s, source_s, own_s = here
    totals = total_ref[...]
    area = joined(info_m[1], first, last, area_s)
    source = joined(info_m[2], first, last, source_s)
    own = joined(info_m[3], first, last, own_s)
    total = joined(info_m[0], first, last, totals) + moved(totals, layout, target)
    residual = total - source
    total_ref[...] = 2.0 * area * residual
    return own * area * residual * residual


def put(ref, parts, base):
    value = functools.reduce(lambda one, two: one + two, parts)
    ref[...] = value if base is None else base[...] + value


def backward(places, groups, total_ref, par_ref, w_ref, d_ref, acc_ref, gw_ref, base):
    w1, w2, pw = par_ref.at[1, 0], par_ref.at[1, 1], par_ref.at[1, 5]

    def start(k, g):
        return acc_ref.at[k] if g else None if base is None else base[0].at[k]

    def cotangents(g):
        d_bases, mixes = [], []
        for row in groups[g]:
            coef_ref, c, _, state_ref, k = places[row]
            c3 = coef_ref[1, 5, c : c + 1, :]
            adjoint = total_ref[row : row + 1, :]
            scale = state_ref[k, 2] * adjoint
            d_base = scale * state_ref[k, 3]
            d_bases.append(d_base)
            mixes.append(state_ref[k, 1] * adjoint)
            d_ref[row, :, 0:LANES] = d_base.astype(BF16)
            d_ref[row, :, LANES : 2 * LANES] = (scale * state_ref[k, 4]).astype(BF16)
            d_ref[row, :, 2 * LANES : 3 * LANES] = (scale * state_ref[k, 5]).astype(BF16)
            d_ref[row, :, 3 * LANES :] = (scale * c3).astype(BF16)
        put(acc_ref.at[4], d_bases, start(4, g))
        put(acc_ref.at[5], mixes, start(5, g))

    cotangents(0)
    for g, group in enumerate(groups):
        d_streams = [
            jnp.dot(w_ref[0, 0], d_ref[row], preferred_element_type=F32) for row in group
        ]
        terms = [
            lax.dot_general(
                places[row][2][places[row][4]],
                d_ref[row],
                (((1,), (1,)), ((), ())),
                preferred_element_type=F32,
            )
            for row in group
        ]
        if g + 1 < len(groups):
            cotangents(g + 1)
        put(gw_ref, terms, gw_ref if g else None if base is None else base[1])
        parts = [[], [], [], []]
        for row, ds in zip(group, d_streams):
            coef_ref, c, _, state_ref, k = places[row]
            xi, eta = coef_ref[1, 0, c : c + 1, :], coef_ref[1, 1, c : c + 1, :]
            h1 = state_ref[k, 0]
            ds0, ds1 = ds[:, 0:LANES], ds[:, LANES : 2 * LANES]
            ds2, ds3 = ds[:, 2 * LANES : 3 * LANES], ds[:, 3 * LANES :]
            d1 = 1.0 - h1 * h1
            cross = w1[...] * ds1 + w2[...] * ds2
            d_pre = d1 * (ds0 + pw[...] * ds3 * (3.0 * d1 - 2.0) - (4.0 * h1) * cross)
            d1x2 = 2.0 * d1
            parts[0].append(d1x2 * ds1 + xi * d_pre)
            parts[1].append(d1x2 * ds2 + eta * d_pre)
            parts[2].append(d_pre)
            parts[3].append(h1 * d1 * ds3)
        for k, part in enumerate(parts):
            put(acc_ref.at[k], part, start(k, g))


def high_kernel(
    mid_ref,
    hi_ref,
    tab_ref,
    w_ref,
    par_ref,
    coef_m,
    info_m,
    s_m,
    state_m,
    acc_ref,
    gw_ref,
    loss_ref,
    coef_ref,
    s_ref,
    state_ref,
    side_par,
    chunk_ref,
    total_ref,
    d_ref,
):
    work = (coef_ref, total_ref, side_par, chunk_ref, s_ref, state_ref)
    here = side(HIGH, 1, mid_ref, hi_ref, tab_ref[...], par_ref, work)
    loss_ref[...] = residuals(info_m, 0, 2, here, total_ref, HIGH, EARLY)
    places = [(coef_m, c, s_m, state_m, c) for c in range(2)]
    places += [(coef_ref, 3 + k, s_ref, state_ref, k) for k in range(2)]
    backward(
        places, ((0, 1, 2, 3),), total_ref, par_ref, w_ref, d_ref, acc_ref, gw_ref, None
    )


def last_kernel(
    mid_ref,
    lo_ref,
    w_ref,
    par_ref,
    coef_m,
    info_m,
    s_m,
    state_m,
    acc_h,
    gw_h,
    loss_h,
    gw_ref,
    gs_ref,
    stat_ref,
    coef_ref,
    s_ref,
    state_ref,
    side_par,
    chunk_ref,
    total_ref,
    d_ref,
    acc_ref,
):
    work = (coef_ref, total_ref, side_par, chunk_ref, s_ref, state_ref)
    here = side(BELOW, -1, mid_ref, lo_ref, None, par_ref, work)
    loss = jnp.sum(
        loss_h[...] + residuals(info_m, 2, 3, here, total_ref, BELOW, LATE)
    )
    places = [(coef_m, 2, s_m, state_m, 2)]
    places += [(coef_ref, 3 + k, s_ref, state_ref, k) for k in range(2)]
    base = (acc_h, gw_h)
    backward(
        places, ((0, 1), (2,)), total_ref, par_ref, w_ref, d_ref, acc_ref, gw_ref, base
    )
    sums = [jnp.sum(acc_ref[k], axis=1, keepdims=True) for k in range(6)]
    turn = -16.0 * sums[3]
    grid = jnp.concatenate(
        [
            sums[0] + turn * par_ref[1, 0, :, 0:1],
            sums[1] + turn * par_ref[1, 1, :, 0:1],
            sums[2],
            sums[4],
            sums[5],
            jnp.zeros((H, 3), F32),
        ],
        axis=1,
    )
    gs_ref[...] = jnp.transpose(grid)
    gw = gw_ref[...]
    square = jnp.sum(gw * gw) + jnp.sum(grid * grid)
    lane = lax.broadcasted_iota(jnp.int32, stat_ref.shape, 2)
    stat_ref[...] = jnp.where(lane == 0, square, jnp.where(lane == 1, loss, 0.0))


def sum_kernel(got_ref, out_ref):
    total = jnp.sum(got_ref[...], axis=0, keepdims=True)
    out_ref[...] = jnp.broadcast_to(total, out_ref.shape)


def scale_kernel(nets, got_ref, gw_ref, gs_ref, o0, o1, o2, o3, o4, loss_ref):
    total = jnp.sum(got_ref[...], axis=0)
    rms = jnp.sqrt(total[:, 0:1] / (nets * (H * H + 5 * H)) + EPS)
    gs = gs_ref[...] / rms
    o0[0, 0] = gs[0:2]
    o1[0] = gs[2:3]
    o2[0, 0] = gw_ref[...] / rms
    o3[0] = gs[3:4]
    o4[0] = gs[4:5]
    loss_ref[...] = total[:, 1:2]


def call(kernel, outs, scratch=(), limit=16 << 20, flops=0, place=pltpu.VMEM):
    extra = {}
    if place != pltpu.VMEM:
        extra["in_specs"] = [pl.BlockSpec(memory_space=place)] * 10
    return pl.pallas_call(
        kernel,
        out_shape=outs,
        scratch_shapes=scratch,
        compiler_params=pltpu.CompilerParams(vmem_limit_bytes=limit),
        cost_estimate=pl.CostEstimate(
            flops=flops, bytes_accessed=1 << 18, transcendentals=0
        ),
        **extra,
    )


def shape(dims, kind=F32):
    return jax.ShapeDtypeStruct(dims, kind)


GX = ("z", "yh", "c")
GY = ("yl", "x")
FIRST = ("z", "c")
SECOND = ("yh", "yl", "x")


def local(
    points,
    diffusion,
    drift,
    ionization,
    source,
    in_weight,
    in_bias,
    mid_weight,
    mid_bias,
    out_weight,
):
    count_x = lax.axis_size(GX)
    count_y = lax.axis_size(GY)
    inputs = (
        points.transpose(1, 2, 0, 3),
        diffusion,
        drift.transpose(1, 2, 0, 3),
        ionization,
        source,
        in_weight,
        in_bias,
        mid_weight,
        mid_bias,
        out_weight,
    )
    payload, table = call(
        pack_kernel,
        (shape((ROWS, H), BF16), shape((8, 384))),
        tuple(pltpu.VMEM(x.shape, x.dtype) for x in inputs)
        + (pltpu.SemaphoreType.DMA((13,)),),
        place=pl.ANY,
        limit=16 << 20,
    )(*(pltpu.with_memory_space_constraint(x, pltpu.HBM) for x in inputs))
    forth = [(i, i + 1) for i in range(count_x - 1)]
    after = lax.ppermute(payload, GX, [(j, i) for i, j in forth])
    before = lax.ppermute(payload, GX, forth)
    row = jnp.stack([after, payload, before])
    pairs = [(i, i ^ 1) for i in range(count_y)]
    bonds = [(i, (i + 1) % count_y) for i in range(1, count_y, 2)]
    above = lax.ppermute(row, GY, pairs)
    below = lax.ppermute(row, GY, bonds + [(j, i) for i, j in bonds])
    first = lax.axis_size(FIRST)
    second = lax.axis_size(SECOND)

    def kept(chunks):
        return ((chunks, H, 4 * LANES), BF16), ((chunks, 6, H, LANES), F32)

    chunk = pltpu.VMEM((8, 8, LANES), F32)
    total = pltpu.VMEM((8, LANES), F32)
    accs = (6, H, LANES)
    params, *middle = call(
        middle_kernel,
        (shape((4, 6, H, LANES)), shape((4, 6, 8, LANES)), shape((4, 8, LANES)))
        + tuple(shape(*k) for k in kept(3)),
        (chunk, total),
        flops=10**9,
    )(row, table)

    def scratch(chunks):
        return (
            pltpu.VMEM((7, 6, 8, LANES), F32),
            *(pltpu.VMEM(*k) for k in kept(2)),
            pltpu.VMEM((3, 6, H, LANES), F32),
            chunk,
            total,
            pltpu.VMEM((chunks, H, 4 * LANES), BF16),
        )

    high = call(
        high_kernel,
        (shape(accs), shape((H, H)), shape((8, LANES))),
        scratch(4),
        limit=20 << 20,
        flops=10**9,
    )(row, above, table, mid_weight, params, *middle)
    grad_w, grad_s, stat = call(
        last_kernel,
        (shape((H, H)), shape((8, H)), shape((first, 1, LANES))),
        scratch(3) + (pltpu.VMEM(accs, F32),),
        limit=20 << 20,
        flops=10**9,
    )(row, below, mid_weight, params, *middle, *high)
    got = lax.all_to_all(stat, FIRST, 0, 0, tiled=True)
    part = call(sum_kernel, shape((second, 1, LANES)))(got)
    got = lax.all_to_all(part, SECOND, 0, 0, tiled=True)
    outs = call(
        lambda *refs: scale_kernel(count_x * count_y, *refs),
        (
            shape((1, 1, 2, H)),
            shape((1, 1, H)),
            shape((1, 1, H, H)),
            shape((1, 1, H)),
            shape((1, 1, H)),
            shape((1, 1)),
        ),
    )(got, grad_w, grad_s)
    return (*outs[:5], outs[5].reshape(()))


def solution(mesh):
    fine = Mesh(
        mesh.devices.reshape(8, 2, 2, 4, 4), ("z", "yh", "c", "yl", "x")
    )
    return jax.shard_map(
        local,
        mesh=fine,
        in_specs=(
            P(None, GX, GY, None),
            P(GX, GY, None),
            P(None, GX, GY, None),
            P(GX, GY, None),
            P(GX, GY, None),
            P(GX, GY, None, None),
            P(GX, GY, None),
            P(GX, GY, None, None),
            P(GX, GY, None),
            P(GX, GY, None),
        ),
        out_specs=(
            P(GX, GY, None, None),
            P(GX, GY, None),
            P(GX, GY, None, None),
            P(GX, GY, None),
            P(GX, GY, None),
            P(),
        ),
        check_vma=False,
    )
```
